32 devices in a mesh: tm: 8 (over z, x), height: 4 (over y, core).
Axes of the slice: x: 2, y: 2, z: 4, core: 2. Of those that a mesh axis runs over, the one named last changes fastest.
Arguments:
- latents: bfloat16 [16, 32, 104, 256], P('tm', 'height'), may hold values from -45 to 45
- first_gain: bfloat16 [256], replicated, may hold values from 0.099609375 to 1.8984375
- first_kernel: bfloat16 [3, 3, 3, 256, 256], replicated, may hold values from -0.078125 to 0.078125
- first_bias: bfloat16 [256], replicated, may hold values from -3 to 3
- second_gain: bfloat16 [256], replicated, may hold values from 0.099609375 to 1.8984375
- second_kernel: bfloat16 [3, 3, 3, 256, 256], replicated, may hold values from -0.078125 to 0.078125
- second_bias: bfloat16 [256], replicated, may hold values from -3 to 3
Outputs:
- decoded: bfloat16 [16, 32, 104, 256], P('tm', 'height')
The draws below stay inside these ranges and needn't reach their ends.
All inputs are finite; a program needn't handle non-finite values.
Results may differ from the reference program's by a relative error of at most 0.0055.
Values may be sent and summed in bfloat16 or wider, within the bound.
No kernel may reach another device: no remote copies, remote signals or barrier semaphores. Data moves between devices by JAX's collectives and lax.ppermute only.
A program may use at most 64 MiB of HBM per device.

```python
import math
import jax
import jax.numpy as jnp
from jax import lax

CH = 256
W = 104
FRAMES = 16
ROWS = 32


def draw_latents(key, part):
    key_base, key_spot, key_chan = jax.random.split(key, 3)
    frame_pos = jnp.arange(FRAMES, dtype=jnp.float32) / max(FRAMES - 1, 1)
    row_pos = jnp.arange(ROWS, dtype=jnp.float32) / max(ROWS - 1, 1)
    ramp = (1.0 + frame_pos)[:, None, None, None] * (1.0 + 0.8 * row_pos)[None, :, None, None]
    base = jnp.clip(jax.random.normal(key_base, (FRAMES, ROWS, W, CH), jnp.float32), -3.5, 3.5)
    spot = jnp.exp(jax.random.uniform(key_spot, (FRAMES, ROWS, W, 1), jnp.float32, 0.0, math.log(3.2)))
    chan = jnp.exp(jax.random.uniform(key_chan, (CH,), jnp.float32, -math.log(3.2), math.log(3.2)))
    return (0.25 * base * ramp * spot * chan).astype(jnp.bfloat16)


def noise(rng, shape, deviation, limit, kind=jnp.bfloat16):
    return jnp.clip(deviation * jax.random.normal(rng, shape, jnp.float32), -limit, limit).astype(kind)


def setup_inputs(seed: int = 0) -> dict:
    keys = jax.random.split(jax.random.key(seed), 8)
    return {
        "latents": draw_latents(jax.random.fold_in(keys[7], 71), 0),
        "first_gain": jnp.clip(1.0 + 0.18 * jax.random.normal(keys[1], (CH,), jnp.float32), 0.099609375, 1.8984375).astype(jnp.bfloat16),
        "first_kernel": noise(keys[2], (3, 3, 3, CH, CH), (27 * CH) ** -0.5, 0.078125),
        "first_bias": noise(keys[3], (CH,), 0.5, 3.0),
        "second_gain": jnp.clip(1.0 + 0.18 * jax.random.normal(keys[4], (CH,), jnp.float32), 0.099609375, 1.8984375).astype(jnp.bfloat16),
        "second_kernel": noise(keys[5], (3, 3, 3, CH, CH), (27 * CH) ** -0.5, 0.078125),
        "second_bias": noise(keys[6], (CH,), 0.5, 3.0),
    }


EPSILON = 1e-06

def normalize(field, gain):
    mean_power = lax.optimization_barrier(jnp.mean(jnp.square(field), axis=-1, keepdims=True))
    return field * lax.rsqrt(mean_power + EPSILON) * gain.astype(jnp.float32)

def activate(field, gain):
    return jax.nn.silu(normalize(field, gain)).astype(jnp.bfloat16)

def causal_conv(acts, kernel, bias):
    padded = jnp.pad(acts, ((2, 0), (1, 1), (1, 1), (0, 0)))
    bias_f = bias.astype(jnp.float32)

    def one_frame(frame_idx):
        total = jnp.zeros((ROWS * W, CH), jnp.float32)
        for tap_time in range(3):
            slab = lax.dynamic_slice_in_dim(padded, frame_idx + tap_time, 1, 0)[0]
            for tap_row in range(3):
                columns = jnp.concatenate([slab[tap_row:tap_row + ROWS, tap_col:tap_col + W] for tap_col in range(3)], -1)
                columns = columns.reshape(ROWS * W, 3 * CH)
                taps = kernel[tap_time, tap_row].reshape(3 * CH, CH)
                total = total + jnp.dot(columns, taps, preferred_element_type=jnp.float32)
        return total.reshape(ROWS, W, CH) + bias_f
    return lax.map(one_frame, jnp.arange(FRAMES, dtype=jnp.int32))

def reference(latents, first_gain, first_kernel, first_bias, second_gain, second_kernel, second_bias):
    field = latents.astype(jnp.float32)
    first_act = activate(field, first_gain)
    first_out = causal_conv(first_act, first_kernel, first_bias).astype(jnp.bfloat16)
    middle = first_out.astype(jnp.float32)
    second_act = activate(middle, second_gain)
    second_out = causal_conv(second_act, second_kernel, second_bias)
    return (field + second_out).astype(jnp.bfloat16)
```

```python
import functools

import jax
import jax.numpy as jnp
from jax import lax
from jax.experimental import pallas as pl
from jax.experimental.pallas import tpu as pltpu
from jax.sharding import PartitionSpec as P

EPSILON = 1e-06
BF16, F32 = jnp.bfloat16, jnp.float32
VMEM_LIMIT = 26 * 2**20
CHUNK = 2


def ring(axis, step):
    peers = lax.axis_size(axis)
    return [(i, (i + step) % peers) for i in range(peers)]


def activate_rows(get_row, gain, shifts, rows, cells):
    for r in range(rows):
        values, mask = get_row(r)
        values = values.astype(F32)
        mean_power = jnp.mean(values * values, axis=-1, keepdims=True)
        normed = values * lax.rsqrt(mean_power + EPSILON) * gain
        act = normed / (1.0 + jnp.exp(-normed))
        if mask is not None:
            act = act * mask
        cell = lax.broadcasted_iota(jnp.int32, act.shape, 0)
        here = slice(r * cells, (r + 1) * cells)
        shifts[0, here, :] = jnp.where(cell == 0, 0.0, pltpu.roll(act, 1, 0))
        shifts[1, here, :] = act
        shifts[2, here, :] = jnp.where(cell == cells - 1, 0.0, pltpu.roll(act, cells - 1, 0))


def pack(shifts, even, odd, rows, cells):
    channels = shifts.shape[-1]
    pair = 2 * cells
    for buf, first, count in ((even, 0, rows // 2), (odd, cells, rows // 2 - 1)):
        for k in range(count):
            for l in range(3):
                buf[k * pair : (k + 1) * pair, l * channels : (l + 1) * channels] = shifts[
                    l, first + k * pair : first + (k + 1) * pair, :
                ].astype(BF16)


def taps(even, odd, kernel, start, length, cells):
    dot = functools.partial(jnp.dot, preferred_element_type=F32)
    lower = 2 * cells + start
    return (
        dot(even[start : start + length], kernel[0, 0])
        + dot(odd[start : start + length], kernel[0, 1])
        + dot(even[lower : lower + length], kernel[0, 2])
    )


def masks():
    row_id, rows = lax.axis_index("height"), lax.axis_size("height")
    above = (row_id > 0).astype(F32)
    below = (row_id < rows - 1).astype(F32)
    before = (lax.axis_index("tm") > 0).astype(F32)
    return above, below, before


def load_frame(frame, up, down, gain, bufs, time_halo):
    shifts, even, odd = bufs
    rows, cells = frame.shape[0], frame.shape[1]
    above, below, before = masks()
    if time_halo:
        above, below = above * before, below * before

    def get_row(r):
        if r == 0:
            return up, above
        if r == rows + 1:
            return down, below
        return frame[r - 1], before if time_halo else None

    activate_rows(get_row, gain[...].astype(F32), shifts, rows + 2, cells)
    pack(shifts, even, odd, rows + 2, cells)


def chunks(rows, cells):
    step = 4 * cells if rows % 4 == 0 else 2 * cells
    return [(s, step) for s in range(0, rows * cells, step)]


def own_kernel(last_ref, first_ref, up, down, gain, k1, k2, acc_first, acc_last, *bufs):
    last, first = last_ref.at[0], first_ref.at[0]
    rows, cells = last.shape[0], last.shape[1]
    even, odd = bufs[1:]
    load_frame(last, up[1], down[1], gain, bufs, False)
    for s, n in chunks(rows, cells):
        acc_last[s : s + n] = taps(even, odd, k2, s, n, cells)
    load_frame(first, up[0], down[0], gain, bufs, False)
    for s, n in chunks(rows, cells):
        acc_last[s : s + n] += taps(even, odd, k1, s, n, cells)
        acc_first[s : s + n] = taps(even, odd, k2, s, n, cells)


def finish(total, bias, residual, out, s, n, cells):
    value = (total + bias[...].astype(F32)).reshape(n // cells, cells, -1)
    r = slice(s // cells, (s + n) // cells)
    if residual is not None:
        value = residual[0, r].astype(F32) + value
    out[0, r] = value.astype(BF16)


def before_kernel(residual, *refs):
    frame, up, down, gain, k0, k1, bias, acc_first, acc_last = refs[:9]
    refs = refs[9:]
    res = None
    if residual:
        res, refs = refs[0], refs[1:]
    out, acc_out = refs[:2]
    refs = refs[2:]
    edges = None
    if not residual:
        edges, refs = refs[0], refs[1:]
    bufs = refs
    frame = frame.at[0]
    rows, cells = frame.shape[0], frame.shape[1]
    even, odd = bufs[1:]
    load_frame(frame, up[0], down[0], gain, bufs, True)
    for s, n in chunks(rows, cells):
        total = acc_last[s : s + n] + taps(even, odd, k0, s, n, cells)
        finish(total, bias, res, out, s, n, cells)
    if edges is not None:
        edges[0, 0] = out[0, 0]
        edges[1, 0] = out[0, rows - 1]
    for s, n in chunks(rows, cells):
        acc_out[s : s + n] = acc_first[s : s + n] + taps(even, odd, k1, s, n, cells)


def earliest_kernel(residual, *refs):
    frame, up, down, gain, k0, bias, acc_first = refs[:7]
    refs = refs[7:]
    res = None
    if residual:
        res, refs = refs[0], refs[2:]
    out, refs = refs[0], refs[1:]
    edges = None
    if not residual:
        edges, refs = refs[0], refs[1:]
    bufs = refs
    frame = frame.at[0]
    rows, cells = frame.shape[0], frame.shape[1]
    even, odd = bufs[1:]
    load_frame(frame, up[0], down[0], gain, bufs, True)
    for s, n in chunks(rows, cells):
        total = acc_first[s : s + n] + taps(even, odd, k0, s, n, cells)
        finish(total, bias, res, out, s, n, cells)
    if edges is not None:
        edges[0, 0] = out[0, 0]
        edges[1, 0] = out[0, rows - 1]


def whole(shape):
    return pl.BlockSpec(tuple(shape), lambda i: (0,) * len(shape))


def part(shape, index):
    return pl.BlockSpec((1, *shape[1:]), lambda i: (index,) + (0,) * (len(shape) - 1))


def call(body, name, units, out_specs, out_shape, args, aliases=None):
    rows, cells, channels = call.block
    flat = (rows + 2) * cells
    arrays = [a for a, _ in args]
    flops = units * 2 * rows * cells * 9 * channels * channels
    return pl.pallas_call(
        body,
        grid=(1,),
        in_specs=[s for _, s in args],
        out_specs=out_specs,
        out_shape=out_shape,
        scratch_shapes=[
            pltpu.VMEM((3, flat, channels), F32),
            pltpu.VMEM((flat, 3 * channels), BF16),
            pltpu.VMEM((flat - 2 * cells, 3 * channels), BF16),
        ],
        input_output_aliases=aliases or {},
        compiler_params=pltpu.CompilerParams(vmem_limit_bytes=VMEM_LIMIT),
        cost_estimate=pl.CostEstimate(
            flops=flops, bytes_accessed=units * 2**21, transcendentals=2 * flat * channels
        ),
        name=name,
    )(*arrays)


def exchange_rows(top, bottom):
    up = lax.ppermute(bottom, "height", ring("height", 1))
    down = lax.ppermute(top, "height", ring("height", -1))
    return up, down


def w(array):
    return array, whole(array.shape)


def section(last, first, edges, gain, kernel, bias, residual):
    rows, cells, channels = call.block
    frame = (1, rows, cells, channels)
    last_frame, first_frame = (a if a.shape[0] == 1 else a[i : i + 1] for (a, _), i in ((last, 1), (first, 0)))
    before = lax.ppermute(last_frame, "tm", ring("tm", 1))
    earliest = lax.ppermute(first_frame, "tm", ring("tm", 1))
    up, down = exchange_rows(*edges)
    acc = jax.ShapeDtypeStruct((rows * cells, channels), F32)
    acc_spec = whole(acc.shape)
    y = jax.ShapeDtypeStruct(frame, BF16)
    edge = jax.ShapeDtypeStruct((2, 1, cells, channels), BF16)
    k = [(kernel, part(kernel.shape, i)) for i in range(3)]
    acc_first, acc_last = call(
        own_kernel, "own", 3, [acc_spec] * 2, [acc] * 2, [last, first, w(up), w(down), w(gain), k[1], k[2]]
    )
    up, down = exchange_rows(before[:, 0], before[:, rows - 1])
    args = [w(before), w(up), w(down), w(gain), k[0], k[1], w(bias), w(acc_first), w(acc_last)]
    body = functools.partial(before_kernel, residual is not None)
    if residual is None:
        y_last, acc_first, edge_last = call(
            body, "before", 2, [whole(frame), acc_spec, whole(edge.shape)], [y, acc, edge], args
        )
    else:
        out = jax.ShapeDtypeStruct(residual.shape, BF16)
        args.append((residual, part(residual.shape, 1)))
        half, acc_first = call(body, "before", 2, [part(out.shape, 1), acc_spec], [out, acc], args)
    up, down = exchange_rows(earliest[:, 0], earliest[:, rows - 1])
    args = [w(earliest), w(up), w(down), w(gain), k[0], w(bias), w(acc_first)]
    body = functools.partial(earliest_kernel, residual is not None)
    if residual is None:
        y_first, edge_first = call(body, "earliest", 1, [whole(frame), whole(edge.shape)], [y, edge], args)
        return y_last, y_first, edge_last, edge_first
    args += [(residual, part(residual.shape, 0)), (half, pl.BlockSpec(memory_space=pl.ANY))]
    return call(body, "earliest", 1, part(out.shape, 0), out, args, {len(args) - 1: 0})


def per_device(
    latents, first_gain, first_kernel, first_bias, second_gain, second_kernel, second_bias
):
    frames, rows, cells, channels = latents.shape
    call.block = (rows, cells, channels)

    def columns(kernel):
        return kernel.reshape(3, 3, 3 * channels, channels)

    edges = latents[:, 0], latents[:, rows - 1]
    lat = [(latents, part(latents.shape, i)) for i in range(2)]
    y_last, y_first, edge_last, edge_first = section(
        lat[1], lat[0], edges, first_gain[None], columns(first_kernel), first_bias[None], None
    )
    edges = [jnp.concatenate([edge_first[i], edge_last[i]]) for i in range(2)]
    return section(
        w(y_last), w(y_first), edges, second_gain[None], columns(second_kernel), second_bias[None], latents
    )


def solution(mesh):
    return jax.shard_map(
        per_device,
        mesh=mesh,
        in_specs=(P("tm", "height", None, None), P(), P(), P(), P(), P(), P()),
        out_specs=P("tm", "height", None, None),
        check_vma=False,
    )
```

```python
import functools

import jax
import jax.numpy as jnp
from jax import lax
from jax.experimental import pallas as pl
from jax.experimental.pallas import tpu as pltpu
from jax.sharding import PartitionSpec as P

EPSILON = 1e-06
BF16, F32 = jnp.bfloat16, jnp.float32
VMEM_LIMIT = 26 * 2**20


def ring(axis, step):
    peers = lax.axis_size(axis)
    return [(i, (i + step) % peers) for i in range(peers)]


def activate_rows(get_row, gain, shifts, rows, cells):
    for r in range(rows):
        values, mask = get_row(r)
        values = values.astype(F32)
        mean_power = jnp.mean(values * values, axis=-1, keepdims=True)
        normed = values * lax.rsqrt(mean_power + EPSILON) * gain
        act = normed / (1.0 + jnp.exp(-normed))
        if mask is not None:
            act = act * mask
        cell = lax.broadcasted_iota(jnp.int32, act.shape, 0)
        here = slice(r * cells, (r + 1) * cells)
        shifts[0, here, :] = jnp.where(cell == 0, 0.0, pltpu.roll(act, 1, 0))
        shifts[1, here, :] = act
        shifts[2, here, :] = jnp.where(cell == cells - 1, 0.0, pltpu.roll(act, cells - 1, 0))


def pack(shifts, even, odd, rows, cells):
    channels = shifts.shape[-1]
    pair = 2 * cells
    for buf, first, count in ((even, 0, rows // 2), (odd, cells, rows // 2 - 1)):
        for k in range(count):
            for l in range(3):
                buf[k * pair : (k + 1) * pair, l * channels : (l + 1) * channels] = shifts[
                    l, first + k * pair : first + (k + 1) * pair, :
                ].astype(BF16)


def taps(even, odd, kernel, start, length, cells):
    dot = functools.partial(jnp.dot, preferred_element_type=F32)
    lower = 2 * cells + start
    return (
        dot(even[start : start + length], kernel[0, 0])
        + dot(odd[start : start + length], kernel[0, 1])
        + dot(even[lower : lower + length], kernel[0, 2])
    )


def masks():
    row_id, rows = lax.axis_index("height"), lax.axis_size("height")
    above = (row_id > 0).astype(F32)
    below = (row_id < rows - 1).astype(F32)
    before = (lax.axis_index("tm") > 0).astype(F32)
    return above, below, before


def load_frame(frame, up, down, gain, bufs, time_halo, edges=None):
    shifts, even, odd = bufs
    rows, cells = frame.shape[0], frame.shape[1]
    if edges is not None:
        rows += 2
    above, below, before = masks()
    if time_halo:
        above, below = above * before, below * before

    def get_row(r):
        if r == 0:
            return up, above
        if r == rows + 1:
            return down, below
        own = before if time_halo else None
        if edges is None:
            return frame[r - 1], own
        if r in (1, rows):
            return edges[0 if r == 1 else 1, 0], own
        return frame[r - 2], own

    activate_rows(get_row, gain[...].astype(F32)[None], shifts, rows + 2, cells)
    pack(shifts, even, odd, rows + 2, cells)


def chunks(rows, cells):
    step = 4 * cells if rows % 4 == 0 else 2 * cells
    return [(s, step) for s in range(0, rows * cells, step)]


def own_kernel(last_ref, first_ref, up, down, gain, k1, k2, acc_first, acc_last, *bufs):
    last, first = last_ref.at[0], first_ref.at[0]
    rows, cells = last.shape[0], last.shape[1]
    even, odd = bufs[1:]
    load_frame(last, up[1], down[1], gain, bufs, False)
    for s, n in chunks(rows, cells):
        acc_last[s : s + n] = taps(even, odd, k2, s, n, cells)
    load_frame(first, up[0], down[0], gain, bufs, False)
    for s, n in chunks(rows, cells):
        acc_last[s : s + n] += taps(even, odd, k1, s, n, cells)
        acc_first[s : s + n] = taps(even, odd, k2, s, n, cells)


def finish(total, bias, residual, out, s, n, cells):
    value = (total + bias[...].astype(F32)[None]).reshape(n // cells, cells, -1)
    r = slice(s // cells, (s + n) // cells)
    if residual is not None:
        value = residual[0, r].astype(F32) + value
    out[0, r] = value.astype(BF16)


def before_kernel(residual, *refs):
    frame, up, down, gain, k0, k1, bias, acc_first, acc_last = refs[:9]
    refs = refs[9:]
    res = None
    if residual:
        res, refs = refs[0], refs[1:]
    out, acc_out = refs[:2]
    refs = refs[2:]
    edges = None
    if not residual:
        edges, refs = refs[0], refs[1:]
    bufs = refs
    frame = frame.at[0]
    rows, cells = frame.shape[0], frame.shape[1]
    even, odd = bufs[1:]
    load_frame(frame, up[0], down[0], gain, bufs, True)
    for s, n in chunks(rows, cells):
        total = acc_last[s : s + n] + taps(even, odd, k0, s, n, cells)
        finish(total, bias, res, out, s, n, cells)
    if edges is not None:
        edges[0, 0] = out[0, 0]
        edges[1, 0] = out[0, rows - 1]
    for s, n in chunks(rows, cells):
        acc_out[s : s + n] = acc_first[s : s + n] + taps(even, odd, k1, s, n, cells)


def earliest_kernel(residual, *refs):
    if residual:
        frame, edges, up, down, gain, k0, bias, acc_first, res, _, out, *bufs = refs
    else:
        frame, up, down, gain, k0, bias, acc_first, out, inner, edges_out, *bufs = refs
        edges = res = None
    rows, cells = out.shape[1], out.shape[2]
    even, odd = bufs[1:]
    load_frame(frame.at[0], up[0], down[0], gain, bufs, True, edges)
    for s, n in chunks(rows, cells):
        total = acc_first[s : s + n] + taps(even, odd, k0, s, n, cells)
        finish(total, bias, res, out, s, n, cells)
    if not residual:
        edges_out[0, 0] = out[0, 0]
        edges_out[1, 0] = out[0, rows - 1]
        inner[0] = out[0, 1 : rows - 1]


def whole(shape):
    return pl.BlockSpec(tuple(shape), lambda i: (0,) * len(shape))


def part(shape, index):
    return pl.BlockSpec((1, *shape[1:]), lambda i: (index,) + (0,) * (len(shape) - 1))


def call(body, name, units, out_specs, out_shape, args, aliases=None):
    rows, cells, channels = call.block
    flat = (rows + 2) * cells
    arrays = [a for a, _ in args]
    flops = units * 2 * rows * cells * 9 * channels * channels
    return pl.pallas_call(
        body,
        grid=(1,),
        in_specs=[s for _, s in args],
        out_specs=out_specs,
        out_shape=out_shape,
        scratch_shapes=[
            pltpu.VMEM((3, flat, channels), F32),
            pltpu.VMEM((flat, 3 * channels), BF16),
            pltpu.VMEM((flat - 2 * cells, 3 * channels), BF16),
        ],
        input_output_aliases=aliases or {},
        compiler_params=pltpu.CompilerParams(vmem_limit_bytes=VMEM_LIMIT),
        cost_estimate=pl.CostEstimate(
            flops=flops, bytes_accessed=units * 2**21, transcendentals=2 * flat * channels
        ),
        name=name,
    )(*arrays)


def exchange_rows(top, bottom):
    up = lax.ppermute(bottom, "height", ring("height", 1))
    down = lax.ppermute(top, "height", ring("height", -1))
    return up, down


def w(array):
    return array, whole(array.shape)


def shift(array):
    return lax.ppermute(array, "tm", ring("tm", 1))


def shapes():
    rows, cells, channels = call.block
    acc = jax.ShapeDtypeStruct((rows * cells, channels), F32)
    frame = jax.ShapeDtypeStruct((1, rows, cells, channels), BF16)
    inner = jax.ShapeDtypeStruct((1, rows - 2, cells, channels), BF16)
    edge = jax.ShapeDtypeStruct((2, 1, cells, channels), BF16)
    return acc, frame, inner, edge


def own(last, first, up, down, gain, k):
    acc = shapes()[0]
    args = [last, first, w(up), w(down), gain, k[1], k[2]]
    return call(own_kernel, "own", 3, [whole(acc.shape)] * 2, [acc, acc], args)


def after(token, blocks, name):
    def copy(*refs):
        count = (len(refs) - 1) // 2
        for source, target in zip(refs[:count], refs[count + 1 :]):
            target[...] = source[...]

    outs = [jax.ShapeDtypeStruct(spec.block_shape, array.dtype) for array, spec in blocks]
    return pl.pallas_call(
        copy,
        grid=(1,),
        in_specs=[spec for _, spec in blocks] + [pl.BlockSpec(memory_space=pl.ANY)],
        out_specs=[whole(o.shape) for o in outs],
        out_shape=outs,
        compiler_params=pltpu.CompilerParams(vmem_limit_bytes=4 * 2**20),
        name=name,
    )(*[array for array, _ in blocks], token)


def rows_after(token, array, places):
    block = (1, 1, *array.shape[2:])
    blocks = [(array, pl.BlockSpec(block, lambda i, p=p: (*p, 0, 0))) for p in places]
    return [a[0] for a in after(token, blocks, "edges")]


def first_section(latents, gain, kernel, bias):
    rows = latents.shape[1]
    acc, frame, inner, edge = shapes()
    k = [(kernel, part(kernel.shape, i)) for i in range(3)]
    last, first = ((latents, part(latents.shape, i)) for i in (1, 0))
    before = shift(latents[1:])
    edges = latents[:, 0], latents[:, rows - 1]
    up, down = exchange_rows(*edges)
    earliest = shift(after(up, [first], "first")[0])
    acc_first, acc_last = own(last, first, up, down, gain, k)
    up, down = exchange_rows(*rows_after(acc_last, before, [(0, 0), (0, rows - 1)]))
    args = [w(before), w(up), w(down), gain, k[0], k[1], bias, w(acc_first), w(acc_last)]
    outs = [frame, acc, edge]
    y_last, acc_first, edge_last = call(
        functools.partial(before_kernel, False), "before", 2, [whole(o.shape) for o in outs], outs, args
    )
    up, down = exchange_rows(earliest[:, 0], earliest[:, rows - 1])
    args = [w(earliest), w(up), w(down), gain, k[0], bias, w(acc_first)]
    outs = [frame, inner, edge]
    y_first, inner_first, edge_first = call(
        functools.partial(earliest_kernel, False), "earliest", 1, [whole(o.shape) for o in outs], outs, args
    )
    return y_last, y_first, edge_last, inner_first, edge_first


def second_section(results, latents, gain, kernel, bias):
    y_last, y_first, edge_last, inner_first, edge_first = results
    rows = latents.shape[1]
    acc = shapes()[0]
    k = [(kernel, part(kernel.shape, i)) for i in range(3)]
    before = shift(y_last)
    earliest_edges = shift(edge_first)
    earliest = shift(inner_first)
    edges = [jnp.concatenate([edge_first[i], edge_last[i]]) for i in range(2)]
    up, down = exchange_rows(*edges)
    acc_first, acc_last = own(w(y_last), w(y_first), up, down, gain, k)
    up, down = exchange_rows(*rows_after(acc_last, before, [(0, 0), (0, rows - 1)]))
    args = [w(before), w(up), w(down), gain, k[0], k[1], bias, w(acc_first), w(acc_last)]
    args.append((latents, part(latents.shape, 1)))
    out = jax.ShapeDtypeStruct(latents.shape, BF16)
    half, acc_first = call(
        functools.partial(before_kernel, True),
        "before",
        2,
        [part(out.shape, 1), whole(acc.shape)],
        [out, acc],
        args,
    )
    up, down = exchange_rows(*rows_after(acc_last, earliest_edges, [(0, 0), (1, 0)]))
    args = [w(earliest), w(earliest_edges), w(up), w(down), gain, k[0], bias, w(acc_first)]
    args += [(latents, part(latents.shape, 0)), (half, pl.BlockSpec(memory_space=pl.ANY))]
    body = functools.partial(earliest_kernel, True)
    return call(body, "earliest", 1, part(out.shape, 0), out, args, {len(args) - 1: 0})


def per_device(
    latents, first_gain, first_kernel, first_bias, second_gain, second_kernel, second_bias
):
    frames, rows, cells, channels = latents.shape
    call.block = (rows, cells, channels)

    def columns(kernel):
        return kernel.reshape(3, 3, 3 * channels, channels)

    first_gain, first_bias, second_gain, second_bias = map(w, (first_gain, first_bias, second_gain, second_bias))
    results = first_section(latents, first_gain, columns(first_kernel), first_bias)
    return second_section(results, latents, second_gain, columns(second_kernel), second_bias)


def solution(mesh):
    return jax.shard_map(
        per_device,
        mesh=mesh,
        in_specs=(P("tm", "height", None, None), P(), P(), P(), P(), P(), P()),
        out_specs=P("tm", "height", None, None),
        check_vma=False,
    )
```

```python
import functools

import jax
import jax.numpy as jnp
from jax import lax
from jax.experimental import pallas as pl
from jax.experimental.pallas import tpu as pltpu
from jax.sharding import PartitionSpec as P

EPSILON = 1e-06
BF16, F32 = jnp.bfloat16, jnp.float32
VMEM_LIMIT = 26 * 2**20


def ring(axis, step):
    peers = lax.axis_size(axis)
    return [(i, (i + step) % peers) for i in range(peers)]


def activate_rows(get_row, gain, shifts, rows, cells):
    for r in range(rows):
        values, mask = get_row(r)
        values = values.astype(F32)
        mean_power = jnp.mean(values * values, axis=-1, keepdims=True)
        normed = values * lax.rsqrt(mean_power + EPSILON) * gain
        act = normed / (1.0 + jnp.exp(-normed))
        if mask is not None:
            act = act * mask
        cell = lax.broadcasted_iota(jnp.int32, act.shape, 0)
        here = slice(r * cells, (r + 1) * cells)
        shifts[0, here, :] = jnp.where(cell == 0, 0.0, pltpu.roll(act, 1, 0))
        shifts[1, here, :] = act
        shifts[2, here, :] = jnp.where(cell == cells - 1, 0.0, pltpu.roll(act, cells - 1, 0))


def pack(shifts, even, odd, rows, cells):
    channels = shifts.shape[-1]
    pair = 2 * cells
    for buf, first, count in ((even, 0, rows // 2), (odd, cells, rows // 2 - 1)):
        for k in range(count):
            for l in range(3):
                buf[k * pair : (k + 1) * pair, l * channels : (l + 1) * channels] = shifts[
                    l, first + k * pair : first + (k + 1) * pair, :
                ].astype(BF16)


def taps(even, odd, kernel, start, length, cells):
    dot = functools.partial(jnp.dot, preferred_element_type=F32)
    lower = 2 * cells + start
    return (
        dot(even[start : start + length], kernel[0, 0])
        + dot(odd[start : start + length], kernel[0, 1])
        + dot(even[lower : lower + length], kernel[0, 2])
    )


def masks():
    row_id, rows = lax.axis_index("height"), lax.axis_size("height")
    above = (row_id > 0).astype(F32)
    below = (row_id < rows - 1).astype(F32)
    return above, below


def load_frame(frame, inward, outward, gain, bufs, edges=None):
    shifts, even, odd = bufs
    rows, cells = frame.shape[0], frame.shape[1]
    if edges is not None:
        rows += 2
    above, below = masks()

    lower = lax.axis_index("height") % 2 == 0

    def get_row(r):
        if r == 0:
            return jnp.where(lower, outward, inward), above
        if r == rows + 1:
            return jnp.where(lower, inward, outward), below
        if edges is None:
            return frame[r - 1], None
        if r in (1, rows):
            return edges[0 if r == 1 else 1, 0], None
        return frame[r - 2], None

    activate_rows(get_row, gain[...].astype(F32)[None], shifts, rows + 2, cells)
    pack(shifts, even, odd, rows + 2, cells)


def chunks(rows, cells):
    step = 4 * cells if rows % 4 == 0 else 2 * cells
    return [(s, step) for s in range(0, rows * cells, step)]


def own_kernel(last_ref, first_ref, up, down, gain, k1, k2, _, acc_first, acc_last, *bufs):
    last, first = last_ref.at[0], first_ref.at[0]
    rows, cells = last.shape[0], last.shape[1]
    even, odd = bufs[1:]
    load_frame(last, up[1], down[1], gain, bufs)
    for s, n in chunks(rows, cells):
        acc_last[s : s + n] = taps(even, odd, k2, s, n, cells)
    load_frame(first, up[0], down[0], gain, bufs)
    for s, n in chunks(rows, cells):
        acc_last[s : s + n] += taps(even, odd, k1, s, n, cells)
        acc_first[s : s + n] = taps(even, odd, k2, s, n, cells)


def finish(total, bias, residual, out, s, n, cells):
    value = (total + bias[...].astype(F32)[None]).reshape(n // cells, cells, -1)
    r = slice(s // cells, (s + n) // cells)
    if residual is not None:
        value = residual[0, r].astype(F32) + value
    out[0, r] = value.astype(BF16)


def frames_before(body):
    first = lax.axis_index("tm") == 0
    pl.when(first)(lambda: body(False))
    pl.when(jnp.logical_not(first))(lambda: body(True))


def before_kernel(residual, *refs):
    frame, up, down, gain, k0, k1, bias, acc_first, acc_last = refs[:9]
    refs = refs[9:]
    res = None
    if residual:
        res, refs = refs[0], refs[1:]
    out, acc_out = refs[:2]
    refs = refs[2:]
    edges = None
    if not residual:
        edges, refs = refs[0], refs[1:]
    bufs = refs
    frame = frame.at[0]
    rows, cells = frame.shape[0], frame.shape[1]
    even, odd = bufs[1:]

    @frames_before
    def _(there):
        if there:
            load_frame(frame, up[0], down[0], gain, bufs)
        for s, n in chunks(rows, cells):
            total = acc_last[s : s + n]
            if there:
                total = total + taps(even, odd, k0, s, n, cells)
            finish(total, bias, res, out, s, n, cells)
        for s, n in chunks(rows, cells):
            total = acc_first[s : s + n]
            if there:
                total = total + taps(even, odd, k1, s, n, cells)
            acc_out[s : s + n] = total

    if edges is not None:
        edges[0, 0] = out[0, 0]
        edges[1, 0] = out[0, rows - 1]


def earliest_kernel(residual, *refs):
    if residual:
        frame, edges, up, down, gain, k0, bias, acc_first, res, _, out, *bufs = refs
    else:
        frame, up, down, gain, k0, bias, acc_first, out, inner, edges_out, *bufs = refs
        edges = res = None
    rows, cells = out.shape[1], out.shape[2]
    even, odd = bufs[1:]

    @frames_before
    def _(there):
        if there:
            load_frame(frame.at[0], up[0], down[0], gain, bufs, edges)
        for s, n in chunks(rows, cells):
            total = acc_first[s : s + n]
            if there:
                total = total + taps(even, odd, k0, s, n, cells)
            finish(total, bias, res, out, s, n, cells)

    if not residual:
        edges_out[0, 0] = out[0, 0]
        edges_out[1, 0] = out[0, rows - 1]
        inner[0] = out[0, 1 : rows - 1]


def whole(shape):
    return pl.BlockSpec(tuple(shape), lambda i: (0,) * len(shape))


def part(shape, index):
    return pl.BlockSpec((1, *shape[1:]), lambda i: (index,) + (0,) * (len(shape) - 1))


def call(body, name, units, out_specs, out_shape, args, aliases=None):
    rows, cells, channels = call.block
    flat = (rows + 2) * cells
    arrays = [a for a, _ in args]
    flops = units * 2 * rows * cells * 9 * channels * channels
    return pl.pallas_call(
        body,
        grid=(1,),
        in_specs=[s for _, s in args],
        out_specs=out_specs,
        out_shape=out_shape,
        scratch_shapes=[
            pltpu.VMEM((3, flat, channels), F32),
            pltpu.VMEM((flat, 3 * channels), BF16),
            pltpu.VMEM((flat - 2 * cells, 3 * channels), BF16),
        ],
        input_output_aliases=aliases or {},
        compiler_params=pltpu.CompilerParams(vmem_limit_bytes=VMEM_LIMIT),
        cost_estimate=pl.CostEstimate(
            flops=flops, bytes_accessed=units * 2**21, transcendentals=2 * flat * channels
        ),
        name=name,
    )(*arrays)


def exchange_rows(inward, outward):
    bands = lax.axis_size("height")
    pairs = [(i, i ^ 1) for i in range(bands)]
    others = [(i, (i + (1 if i % 2 else -1)) % bands) for i in range(bands)]
    outward = lax.ppermute(outward, "height", others)
    return lax.ppermute(inward, "height", pairs), outward


def w(array):
    return array, whole(array.shape)


def shift(array):
    return lax.ppermute(array, "tm", ring("tm", 1))


def shapes():
    rows, cells, channels = call.block
    acc = jax.ShapeDtypeStruct((rows * cells, channels), F32)
    frame = jax.ShapeDtypeStruct((1, rows, cells, channels), BF16)
    inner = jax.ShapeDtypeStruct((1, rows - 2, cells, channels), BF16)
    edge = jax.ShapeDtypeStruct((2, 1, cells, channels), BF16)
    return acc, frame, inner, edge


def own(last, first, up, down, gain, k, token):
    acc = shapes()[0]
    args = [last, first, w(up), w(down), gain, k[1], k[2], (token, pl.BlockSpec(memory_space=pl.ANY))]
    return call(own_kernel, "own", 3, [whole(acc.shape)] * 2, [acc, acc], args)


def after(token, blocks, name):
    def copy(*refs):
        count = (len(refs) - 1) // 2
        for source, target in zip(refs[:count], refs[count + 1 :]):
            target[...] = source[...]

    outs = [jax.ShapeDtypeStruct(spec.block_shape, array.dtype) for array, spec in blocks]
    return pl.pallas_call(
        copy,
        grid=(1,),
        in_specs=[spec for _, spec in blocks] + [pl.BlockSpec(memory_space=pl.ANY)],
        out_specs=[whole(o.shape) for o in outs],
        out_shape=outs,
        compiler_params=pltpu.CompilerParams(vmem_limit_bytes=4 * 2**20),
        name=name,
    )(*[array for array, _ in blocks], token)


def rows_after(token, *sources):
    def copy(*refs):
        count = len(sources)
        inward, outward = refs[-2:]
        lower = lax.axis_index("height") % 2 == 0
        for n in range(count):
            top, bottom = (ref.reshape(inward.shape[1:])[...] for ref in refs[2 * n : 2 * n + 2])
            inward[n] = jnp.where(lower, bottom, top)
            outward[n] = jnp.where(lower, top, bottom)

    args = []
    for array, *places in sources:
        for place in places:
            block = (1,) * len(place) + array.shape[len(place) :]
            tail = (0,) * (array.ndim - len(place))
            args.append((array, pl.BlockSpec(block, lambda i, p=place, t=tail: (*p, *t))))
    out = jax.ShapeDtypeStruct((len(sources), *sources[0][0].shape[-2:]), BF16)
    return pl.pallas_call(
        copy,
        grid=(1,),
        in_specs=[spec for _, spec in args] + [pl.BlockSpec(memory_space=pl.ANY)],
        out_specs=[whole(out.shape)] * 2,
        out_shape=[out] * 2,
        compiler_params=pltpu.CompilerParams(vmem_limit_bytes=4 * 2**20),
        name="edges",
    )(*[array for array, _ in args], token)


def first_section(latents, gain, kernel, bias):
    rows = latents.shape[1]
    acc, frame, inner, edge = shapes()
    k = [(kernel, part(kernel.shape, i)) for i in range(3)]
    last, first = ((latents, part(latents.shape, i)) for i in (1, 0))
    before = shift(latents[1:])
    bottom = rows - 1
    up, down = exchange_rows(*rows_after(gain[0], (latents, (0, 0), (0, bottom)), (latents, (1, 0), (1, bottom))))
    earliest = shift(after(up, [first], "first")[0])
    before_edges = rows_after(up, (before, (0, 0), (0, bottom)))
    acc_first, acc_last = own(last, first, up, down, gain, k, before_edges[0])
    up, down = exchange_rows(*before_edges)
    args = [w(before), w(up), w(down), gain, k[0], k[1], bias, w(acc_first), w(acc_last)]
    outs = [frame, acc, edge]
    y_last, acc_first, edge_last = call(
        functools.partial(before_kernel, False), "before", 2, [whole(o.shape) for o in outs], outs, args
    )
    up, down = exchange_rows(*rows_after(y_last, (earliest, (0, 0), (0, bottom))))
    args = [w(earliest), w(up), w(down), gain, k[0], bias, w(acc_first)]
    outs = [frame, inner, edge]
    y_first, inner_first, edge_first = call(
        functools.partial(earliest_kernel, False), "earliest", 1, [whole(o.shape) for o in outs], outs, args
    )
    return y_last, y_first, edge_last, inner_first, edge_first


def second_section(results, latents, gain, kernel, bias):
    y_last, y_first, edge_last, inner_first, edge_first = results
    rows = latents.shape[1]
    acc = shapes()[0]
    k = [(kernel, part(kernel.shape, i)) for i in range(3)]
    before = shift(y_last)
    earliest_edges = shift(edge_first)
    earliest = shift(inner_first)
    up, down = exchange_rows(*rows_after(edge_first, (edge_first, (0,), (1,)), (edge_last, (0,), (1,))))
    before_edges = rows_after(up, (before, (0, 0), (0, rows - 1)))
    acc_first, acc_last = own(w(y_last), w(y_first), up, down, gain, k, before_edges[0])
    up, down = exchange_rows(*before_edges)
    args = [w(before), w(up), w(down), gain, k[0], k[1], bias, w(acc_first), w(acc_last)]
    args.append((latents, part(latents.shape, 1)))
    out = jax.ShapeDtypeStruct(latents.shape, BF16)
    half, acc_first = call(
        functools.partial(before_kernel, True),
        "before",
        2,
        [part(out.shape, 1), whole(acc.shape)],
        [out, acc],
        args,
    )
    up, down = exchange_rows(*rows_after(acc_last, (earliest_edges, (0,), (1,))))
    args = [w(earliest), w(earliest_edges), w(up), w(down), gain, k[0], bias, w(acc_first)]
    args += [(latents, part(latents.shape, 0)), (half, pl.BlockSpec(memory_space=pl.ANY))]
    body = functools.partial(earliest_kernel, True)
    return call(body, "earliest", 1, part(out.shape, 0), out, args, {len(args) - 1: 0})


def per_device(
    latents, first_gain, first_kernel, first_bias, second_gain, second_kernel, second_bias
):
    frames, rows, cells, channels = latents.shape
    call.block = (rows, cells, channels)

    def columns(kernel):
        return kernel.reshape(3, 3, 3 * channels, channels)

    first_gain, first_bias, second_gain, second_bias = map(w, (first_gain, first_bias, second_gain, second_bias))
    results = first_section(latents, first_gain, columns(first_kernel), first_bias)
    return second_section(results, latents, second_gain, columns(second_kernel), second_bias)


def solution(mesh):
    return jax.shard_map(
        per_device,
        mesh=mesh,
        in_specs=(P("tm", "height", None, None), P(), P(), P(), P(), P(), P()),
        out_specs=P("tm", "height", None, None),
        check_vma=False,
    )
```

```python
import functools

import jax
import jax.numpy as jnp
from jax import lax
from jax.experimental import pallas as pl
from jax.experimental.pallas import tpu as pltpu
from jax.sharding import PartitionSpec as P

EPSILON = 1e-06
BF16, F32 = jnp.bfloat16, jnp.float32
VMEM_LIMIT = 26 * 2**20


def ring(axis, step):
    peers = lax.axis_size(axis)
    return [(i, (i + step) % peers) for i in range(peers)]


def activate_rows(get_row, gain, shifts, rows, cells):
    for r in range(rows):
        values, mask = get_row(r)
        here = slice(r * cells, (r + 1) * cells)
        values = values.astype(F32)
        mean_power = jnp.mean(values * values, axis=-1, keepdims=True)
        normed = values * lax.rsqrt(mean_power + EPSILON) * gain
        act = normed / (1.0 + jnp.exp(-normed))
        if mask is not None:
            act = act * mask
        cell = lax.broadcasted_iota(jnp.int32, act.shape, 0)
        shifts[0, here, :] = jnp.where(cell == 0, 0.0, pltpu.roll(act, 1, 0))
        shifts[1, here, :] = act
        shifts[2, here, :] = jnp.where(cell == cells - 1, 0.0, pltpu.roll(act, cells - 1, 0))


def pack(shifts, even, odd, rows, cells):
    channels = shifts.shape[-1]
    pair = 2 * cells
    for buf, first, count in ((even, 0, rows // 2), (odd, cells, rows // 2 - 1)):
        for k in range(count):
            for l in range(3):
                buf[k * pair : (k + 1) * pair, l * channels : (l + 1) * channels] = shifts[
                    l, first + k * pair : first + (k + 1) * pair, :
                ].astype(BF16)


def taps(even, odd, kernel, start, length, cells):
    dot = functools.partial(jnp.dot, preferred_element_type=F32)
    lower = 2 * cells + start
    return (
        dot(even[start : start + length], kernel[0, 0])
        + dot(odd[start : start + length], kernel[0, 1])
        + dot(even[lower : lower + length], kernel[0, 2])
    )


def masks():
    row_id, rows = lax.axis_index("height"), lax.axis_size("height")
    above = (row_id > 0).astype(F32)
    below = (row_id < rows - 1).astype(F32)
    return above, below


def load_frame(frame, inward, outward, gain, bufs, edges=None):
    shifts, even, odd = bufs
    rows, cells = frame.shape[0], frame.shape[1]
    if edges is not None:
        rows += 2
    above, below = masks()

    lower = lax.axis_index("height") % 2 == 0

    def get_row(r):
        if r == 0:
            return jnp.where(lower, outward, inward), above
        if r == rows + 1:
            return jnp.where(lower, inward, outward), below
        if edges is None:
            return frame[r - 1], None
        if r in (1, rows):
            return edges[0 if r == 1 else 1], None
        return frame[r - 2], None

    activate_rows(get_row, gain[...].astype(F32)[None], shifts, rows + 2, cells)
    pack(shifts, even, odd, rows + 2, cells)


def chunks(rows, cells, fine=False):
    step = 4 * cells if rows % 4 == 0 and not fine else 2 * cells
    return [(s, step) for s in range(0, rows * cells, step)]


def own_kernel(last, first, up, down, gain, k1, k2, _, acc_first, acc_last, *bufs):
    rows, cells = last.shape[1], last.shape[2]
    even, odd = bufs[1:]
    load_frame(last.at[0], up[1], down[1], gain, bufs)
    for s, n in chunks(rows, cells):
        acc_last[s : s + n] = taps(even, odd, k2, s, n, cells)
    load_frame(first.at[0], up[0], down[0], gain, bufs)
    for s, n in chunks(rows, cells):
        acc_last[s : s + n] += taps(even, odd, k1, s, n, cells)
        acc_first[s : s + n] = taps(even, odd, k2, s, n, cells)


def own_last_kernel(last, up, down, gain, k2, _, acc_last, *bufs):
    rows, cells = last.shape[1], last.shape[2]
    even, odd = bufs[1:]
    load_frame(last.at[0], up[0], down[0], gain, bufs)
    for s, n in chunks(rows, cells):
        acc_last[s : s + n] = taps(even, odd, k2, s, n, cells)


def own_first_kernel(first, up, down, gain, k1, k2, acc_in, _, acc_first, acc_last, *bufs):
    rows, cells = first.shape[1], first.shape[2]
    even, odd = bufs[1:]
    load_frame(first.at[0], up[0], down[0], gain, bufs)
    for s, n in chunks(rows, cells):
        acc_last[s : s + n] = acc_in[s : s + n] + taps(even, odd, k1, s, n, cells)
        acc_first[s : s + n] = taps(even, odd, k2, s, n, cells)


def finish(total, bias, s, n, cells):
    value = (total + bias[...].astype(F32)[None]).reshape(n // cells, cells, -1)
    return slice(s // cells, (s + n) // cells), value


class Result:
    def __init__(self, latents, out, frame, rows, sems):
        self.residual, self.out, self.frame, self.rows, self.sems = latents.at[0], out, frame, rows, sems

    def copy(self, s, n, cells):
        r = pl.ds(s // cells, n // cells)
        return pltpu.make_async_copy(
            self.rows.at[r], self.out.at[self.frame, r], self.sems.at[s // n]
        )

    def finish(self, total, bias, s, n, cells):
        r, value = finish(total, bias, s, n, cells)
        self.rows[r] = (self.residual[r].astype(F32) + value).astype(BF16)
        self.copy(s, n, cells).start()

    def wait(self, parts):
        for s, n in parts:
            self.copy(s, n, self.rows.shape[1]).wait()


def frames_before(body):
    first = lax.axis_index("tm") == 0
    pl.when(first)(lambda: body(False))
    pl.when(jnp.logical_not(first))(lambda: body(True))


def before_kernel(residual, *refs):
    if residual:
        frame, up, down, gain, k0, k1, bias, acc_first, acc_last, latents, out, acc_out, *bufs, new, sems = refs
        frame, edges = frame.at[0], None
        result = Result(latents, out, 1, new, sems)
    else:
        frame, edges, up, down, gain, k0, k1, bias, acc_first, acc_last, out, acc_out, *bufs = refs
        frame = frame.at[0]
    cells = up.shape[1]
    rows = acc_first.shape[0] // cells
    even, odd = bufs[1:]

    @frames_before
    def _(there):
        if there:
            load_frame(frame, up[0], down[0], gain, bufs, edges)
        for s, n in chunks(rows, cells):
            total = acc_last[s : s + n]
            if there:
                total = total + taps(even, odd, k0, s, n, cells)
            if residual:
                result.finish(total, bias, s, n, cells)
            else:
                r, value = finish(total, bias, s, n, cells)
                out[0, r] = value.astype(BF16)
        for s, n in chunks(rows, cells):
            total = acc_first[s : s + n]
            if there:
                total = total + taps(even, odd, k1, s, n, cells)
            acc_out[s : s + n] = total

    if residual:
        result.wait(chunks(rows, cells))


def earliest_kernel(residual, *refs):
    if residual:
        frame, edges, up, down, gain, k0, bias, acc_first, latents, _, out, *bufs, new, sems = refs
        result = Result(latents, out, 0, new, sems)
    else:
        frame, edges, up, down, gain, k0, bias, acc_first, out, inner, edges_out, *bufs = refs
    cells = up.shape[1]
    rows = acc_first.shape[0] // cells
    even, odd = bufs[1:]

    @frames_before
    def _(there):
        if there:
            load_frame(frame.at[0], up[0], down[0], gain, bufs, edges)
        for s, n in chunks(rows, cells, residual):
            total = acc_first[s : s + n]
            if there:
                total = total + taps(even, odd, k0, s, n, cells)
            if residual:
                result.finish(total, bias, s, n, cells)
            else:
                r, value = finish(total, bias, s, n, cells)
                out[0, r] = value.astype(BF16)

    if residual:
        result.wait(chunks(rows, cells, True))
    else:
        edges_out[0] = out[0, 0]
        edges_out[1] = out[0, rows - 1]
        inner[0] = out[0, 1 : rows - 1]


def whole(shape):
    return pl.BlockSpec(tuple(shape), lambda i: (0,) * len(shape))


def part(shape, index):
    return pl.BlockSpec((1, *shape[1:]), lambda i: (index,) + (0,) * (len(shape) - 1))


def call(body, name, units, out_specs, out_shape, args, aliases=None, extra=()):
    rows, cells, channels = call.block
    flat = (rows + 2) * cells
    arrays = [a for a, _ in args]
    flops = units * 2 * rows * cells * 9 * channels * channels
    return pl.pallas_call(
        body,
        grid=(1,),
        in_specs=[s for _, s in args],
        out_specs=out_specs,
        out_shape=out_shape,
        scratch_shapes=[
            pltpu.VMEM((3, flat, channels), F32),
            pltpu.VMEM((flat, 3 * channels), BF16),
            pltpu.VMEM((flat - 2 * cells, 3 * channels), BF16),
            *extra,
        ],
        input_output_aliases=aliases or {},
        compiler_params=pltpu.CompilerParams(vmem_limit_bytes=VMEM_LIMIT),
        cost_estimate=pl.CostEstimate(
            flops=flops, bytes_accessed=units * 2**21, transcendentals=2 * flat * channels
        ),
        name=name,
    )(*arrays)


def exchange_rows(inward, outward):
    bands = lax.axis_size("height")
    pairs = [(i, i ^ 1) for i in range(bands)]
    others = [(i, (i + (1 if i % 2 else -1)) % bands) for i in range(bands)]
    outward = lax.ppermute(outward, "height", others)
    return lax.ppermute(inward, "height", pairs), outward


def w(array):
    return array, whole(array.shape)


def shift(array, closed=True):
    route = ring("tm", 1)
    return lax.ppermute(array, "tm", route if closed else route[:-1])


def shapes():
    rows, cells, channels = call.block
    acc = jax.ShapeDtypeStruct((rows * cells, channels), F32)
    frame = jax.ShapeDtypeStruct((1, rows, cells, channels), BF16)
    inner = jax.ShapeDtypeStruct((1, rows - 2, cells, channels), BF16)
    edge = jax.ShapeDtypeStruct((2, cells, channels), BF16)
    return acc, frame, inner, edge


def own(last, first, up, down, gain, k, token):
    acc = shapes()[0]
    args = [last, first, w(up), w(down), gain, k[1], k[2], (token, pl.BlockSpec(memory_space=pl.ANY))]
    return call(own_kernel, "own", 3, [whole(acc.shape)] * 2, [acc, acc], args)


def own_apart(last, first, up, down, gain, k, early, late):
    acc = shapes()[0]
    up, down = pairs(up, 1), pairs(down, 1)
    args = [last, up[1], down[1], gain, k[2], (early, pl.BlockSpec(memory_space=pl.ANY))]
    acc_last = call(own_last_kernel, "last", 1, [whole(acc.shape)], [acc], args)[0]
    args = [first, up[0], down[0], gain, k[1], k[2], w(acc_last), (late, pl.BlockSpec(memory_space=pl.ANY))]
    return call(own_first_kernel, "first", 2, [whole(acc.shape)] * 2, [acc, acc], args)


def inner_rows(latents, token):
    rows = latents.shape[1]
    inner = shapes()[2]

    def copy(last, first, _, last_out, first_out):
        last_out[...] = last[:, 1 : rows - 1]
        first_out[...] = first[:, 1 : rows - 1]

    return pl.pallas_call(
        copy,
        grid=(1,),
        in_specs=[part(latents.shape, 1), part(latents.shape, 0), pl.BlockSpec(memory_space=pl.ANY)],
        out_specs=[whole(inner.shape)] * 2,
        out_shape=[inner] * 2,
        compiler_params=pltpu.CompilerParams(vmem_limit_bytes=6 * 2**20),
        name="inner",
    )(latents, latents, token)


def rows_after(token, *sources, plain=False):
    count = len(sources)

    def copy(*refs):
        inward, outward, *rows = refs[2 * count + (token is not None) :]
        lower = lax.axis_index("height") % 2 == 0
        for n in range(count):
            top, bottom = (ref.reshape(inward.shape[1:])[...] for ref in refs[2 * n : 2 * n + 2])
            inward[n] = jnp.where(lower, bottom, top)
            outward[n] = jnp.where(lower, top, bottom)
            if plain:
                rows[0][2 * n] = top
                rows[0][2 * n + 1] = bottom

    args = []
    for array, *places in sources:
        for place in places:
            block = (1,) * len(place) + array.shape[len(place) :]
            tail = (0,) * (array.ndim - len(place))
            args.append((array, pl.BlockSpec(block, lambda i, p=place, t=tail: (*p, *t))))
    if token is not None:
        args.append((token, pl.BlockSpec(memory_space=pl.ANY)))
    row = sources[0][0].shape[-2:]
    outs = [jax.ShapeDtypeStruct((n, *row), BF16) for n in [count] * 2 + [2 * count] * plain]
    return pl.pallas_call(
        copy,
        grid=(1,),
        in_specs=[spec for _, spec in args],
        out_specs=[whole(o.shape) for o in outs],
        out_shape=outs,
        compiler_params=pltpu.CompilerParams(vmem_limit_bytes=4 * 2**20),
        name="edges",
    )(*[array for array, _ in args])


def pairs(array, size):
    block = (size, *array.shape[1:])
    return [
        (array, pl.BlockSpec(block, lambda i, n=n: (n,) + (0,) * (len(block) - 1)))
        for n in range(array.shape[0] // size)
    ]


def first_section(latents, gain, kernel, bias):
    bottom = latents.shape[1] - 1
    acc, frame, inner, edge = shapes()
    k = [(kernel, part(kernel.shape, i)) for i in range(3)]
    first, last = ((latents, part(latents.shape, i)) for i in range(2))
    sources = [(latents, (i, 0), (i, bottom)) for i in range(2)]
    *sides, edges = rows_after(None, *sources, plain=True)
    edges = shift(edges)
    up, down = exchange_rows(*sides)
    inner_last, inner_first = inner_rows(latents, sides[0])
    before, earliest = shift(inner_last), shift(inner_first, False)

    sides = rows_after(up, (edges, (2,), (3,)), (edges, (0,), (1,)))
    acc_first, acc_last = own(last, first, up, down, gain, k, sides[0])
    up, down = (pairs(a, 1) for a in exchange_rows(*sides))
    edges = pairs(edges, 2)
    outs = [frame, acc]
    y_last, acc_first = call(
        functools.partial(before_kernel, False),
        "before",
        2,
        [whole(o.shape) for o in outs],
        outs,
        [w(before), edges[1], up[0], down[0], gain, k[0], k[1], bias, w(acc_first), w(acc_last)],
    )
    outs = [frame, inner, edge]
    y_first, inner_first, edge_first = call(
        functools.partial(earliest_kernel, False),
        "earliest",
        1,
        [whole(o.shape) for o in outs],
        outs,
        [w(earliest), edges[0], up[1], down[1], gain, k[0], bias, w(acc_first)],
    )
    return y_last, y_first, inner_first, edge_first


def second_section(results, latents, gain, kernel, bias):
    y_last, y_first, inner_first, edge_first = results
    bottom = latents.shape[1] - 1
    acc = shapes()[0]
    k = [(kernel, part(kernel.shape, i)) for i in range(3)]
    before = shift(y_last)
    edges = shift(edge_first)
    earliest = shift(inner_first)
    up, down = exchange_rows(
        *rows_after(edge_first, (y_first, (0, 0), (0, bottom)), (y_last, (0, 0), (0, bottom)))
    )
    sides = rows_after(up, (before, (0, 0), (0, bottom)))
    acc_first, acc_last = own_apart(w(y_last), w(y_first), up, down, gain, k, up, sides[0])

    out = jax.ShapeDtypeStruct(latents.shape, BF16)
    anywhere = pl.BlockSpec(memory_space=pl.ANY)
    extra = [pltpu.VMEM(latents.shape[1:], BF16), pltpu.SemaphoreType.DMA((len(chunks(*latents.shape[1:3], True)),))]
    args = [w(before), *map(w, exchange_rows(*sides)), gain, k[0], k[1], bias, w(acc_first), w(acc_last)]
    args.append((latents, part(latents.shape, 1)))
    half, acc_first = call(
        functools.partial(before_kernel, True),
        "before",
        2,
        [anywhere, whole(acc.shape)],
        [out, acc],
        args,
        extra=extra,
    )
    sides = rows_after(acc_last, (edges, (0,), (1,)))
    args = [w(earliest), w(edges), *map(w, exchange_rows(*sides)), gain, k[0], bias, w(acc_first)]
    args += [(latents, part(latents.shape, 0)), (half, anywhere)]
    body = functools.partial(earliest_kernel, True)
    return call(body, "earliest", 1, anywhere, out, args, {len(args) - 1: 0}, extra)


def per_device(
    latents, first_gain, first_kernel, first_bias, second_gain, second_kernel, second_bias
):
    frames, rows, cells, channels = latents.shape
    call.block = (rows, cells, channels)

    def columns(kernel):
        return kernel.reshape(3, 3, 3 * channels, channels)

    first_gain, first_bias, second_gain, second_bias = map(w, (first_gain, first_bias, second_gain, second_bias))
    results = first_section(latents, first_gain, columns(first_kernel), first_bias)
    return second_section(results, latents, second_gain, columns(second_kernel), second_bias)


def solution(mesh):
    return jax.shard_map(
        per_device,
        mesh=mesh,
        in_specs=(P("tm", "height", None, None), P(), P(), P(), P(), P(), P()),
        out_specs=P("tm", "height", None, None),
        check_vma=False,
    )
```

```python
import functools

import jax
import jax.numpy as jnp
from jax import lax
from jax.experimental import pallas as pl
from jax.experimental.pallas import tpu as pltpu
from jax.sharding import PartitionSpec as P

EPSILON = 1e-06
BF16, F32 = jnp.bfloat16, jnp.float32
VMEM_LIMIT = 26 * 2**20


def ring(axis, step):
    peers = lax.axis_size(axis)
    return [(i, (i + step) % peers) for i in range(peers)]


def activate_rows(get_row, gain, shifts, rows, cells):
    for r in range(rows):
        values, mask = get_row(r)
        here = slice(r * cells, (r + 1) * cells)
        values = values.astype(F32)
        mean_power = jnp.mean(values * values, axis=-1, keepdims=True)
        normed = values * lax.rsqrt(mean_power + EPSILON) * gain
        act = normed / (1.0 + jnp.exp(-normed))
        if mask is not None:
            act = act * mask
        cell = lax.broadcasted_iota(jnp.int32, act.shape, 0)
        shifts[0, here, :] = jnp.where(cell == 0, 0.0, pltpu.roll(act, 1, 0))
        shifts[1, here, :] = act
        shifts[2, here, :] = jnp.where(cell == cells - 1, 0.0, pltpu.roll(act, cells - 1, 0))


def pack(shifts, even, odd, rows, cells):
    channels = shifts.shape[-1]
    pair = 2 * cells
    for buf, first, count in ((even, 0, rows // 2), (odd, cells, rows // 2 - 1)):
        for k in range(count):
            for l in range(3):
                buf[k * pair : (k + 1) * pair, l * channels : (l + 1) * channels] = shifts[
                    l, first + k * pair : first + (k + 1) * pair, :
                ].astype(BF16)


def taps(even, odd, kernel, start, length, cells):
    dot = functools.partial(jnp.dot, preferred_element_type=F32)
    lower = 2 * cells + start
    return (
        dot(even[start : start + length], kernel[0, 0])
        + dot(odd[start : start + length], kernel[0, 1])
        + dot(even[lower : lower + length], kernel[0, 2])
    )


def masks():
    row_id, rows = lax.axis_index("height"), lax.axis_size("height")
    above = (row_id > 0).astype(F32)
    below = (row_id < rows - 1).astype(F32)
    return above, below


def load_frame(frame, inward, outward, gain, bufs, edges=None):
    shifts, even, odd = bufs
    rows, cells = frame.shape[0], frame.shape[1]
    if edges is not None:
        rows += 2
    above, below = masks()

    lower = lax.axis_index("height") % 2 == 0

    def get_row(r):
        if r == 0:
            return jnp.where(lower, outward, inward), above
        if r == rows + 1:
            return jnp.where(lower, inward, outward), below
        if edges is None:
            return frame[r - 1], None
        if r in (1, rows):
            return edges[0 if r == 1 else 1], None
        return frame[r - 2], None

    activate_rows(get_row, gain[...].astype(F32)[None], shifts, rows + 2, cells)
    pack(shifts, even, odd, rows + 2, cells)


def chunks(rows, cells, fine=False):
    step = 4 * cells if rows % 4 == 0 and not fine else 2 * cells
    return [(s, step) for s in range(0, rows * cells, step)]


def own_kernel(last, first, up, down, gain, k1, k2, _, acc_first, acc_last, *bufs):
    rows, cells = last.shape[1], last.shape[2]
    even, odd = bufs[1:]
    load_frame(last.at[0], up[1], down[1], gain, bufs)
    for s, n in chunks(rows, cells):
        acc_last[s : s + n] = taps(even, odd, k2, s, n, cells)
    load_frame(first.at[0], up[0], down[0], gain, bufs)
    for s, n in chunks(rows, cells):
        acc_last[s : s + n] += taps(even, odd, k1, s, n, cells)
        acc_first[s : s + n] = taps(even, odd, k2, s, n, cells)


def own_last_kernel(last, up, down, gain, k2, _, acc_last, *bufs):
    rows, cells = last.shape[1], last.shape[2]
    even, odd = bufs[1:]
    load_frame(last.at[0], up[0], down[0], gain, bufs)
    for s, n in chunks(rows, cells):
        acc_last[s : s + n] = taps(even, odd, k2, s, n, cells)


def own_first_kernel(first, up, down, gain, k1, k2, acc_in, _, acc_first, acc_last, *bufs):
    rows, cells = first.shape[1], first.shape[2]
    even, odd = bufs[1:]
    load_frame(first.at[0], up[0], down[0], gain, bufs)
    for s, n in chunks(rows, cells):
        acc_last[s : s + n] = acc_in[s : s + n] + taps(even, odd, k1, s, n, cells)
        acc_first[s : s + n] = taps(even, odd, k2, s, n, cells)


def finish(total, bias, s, n, cells):
    value = (total + bias[...].astype(F32)[None]).reshape(n // cells, cells, -1)
    return slice(s // cells, (s + n) // cells), value


class Result:
    def __init__(self, latents, out, frame, rows, sems):
        self.residual, self.out, self.frame, self.rows, self.sems = latents.at[0], out, frame, rows, sems

    def copy(self, s, n, cells):
        r = pl.ds(s // cells, n // cells)
        return pltpu.make_async_copy(
            self.rows.at[r], self.out.at[self.frame, r], self.sems.at[s // n]
        )

    def finish(self, total, bias, s, n, cells):
        r, value = finish(total, bias, s, n, cells)
        self.rows[r] = (self.residual[r].astype(F32) + value).astype(BF16)
        self.copy(s, n, cells).start()

    def wait(self, parts):
        for s, n in parts:
            self.copy(s, n, self.rows.shape[1]).wait()


def frames_before(body):
    first = lax.axis_index("tm") == 0
    pl.when(first)(lambda: body(False))
    pl.when(jnp.logical_not(first))(lambda: body(True))


def before_kernel(residual, *refs):
    if residual:
        frame, up, down, gain, k0, k1, bias, acc_first, acc_last, latents, out, acc_out, *bufs, new, sems = refs
        frame, edges = frame.at[0], None
        result = Result(latents, out, 1, new, sems)
    else:
        frame, edges, up, down, gain, k0, k1, bias, acc_first, acc_last, out, acc_out, *bufs = refs
        frame = frame.at[0]
    cells = up.shape[1]
    rows = acc_first.shape[0] // cells
    even, odd = bufs[1:]

    @frames_before
    def _(there):
        if there:
            load_frame(frame, up[0], down[0], gain, bufs, edges)
        for s, n in chunks(rows, cells):
            total = acc_last[s : s + n]
            if there:
                total = total + taps(even, odd, k0, s, n, cells)
            if residual:
                result.finish(total, bias, s, n, cells)
            else:
                r, value = finish(total, bias, s, n, cells)
                out[0, r] = value.astype(BF16)
        for s, n in chunks(rows, cells):
            total = acc_first[s : s + n]
            if there:
                total = total + taps(even, odd, k1, s, n, cells)
            acc_out[s : s + n] = total

    if residual:
        result.wait(chunks(rows, cells))


def earliest_kernel(residual, *refs):
    if residual:
        frame, edges, up, down, gain, k0, bias, acc_first, latents, _, out, *bufs, new, sems = refs
        result = Result(latents, out, 0, new, sems)
    else:
        frame, edges, up, down, gain, k0, bias, acc_first, out, inner, edges_out, *bufs = refs
    cells = up.shape[1]
    rows = acc_first.shape[0] // cells
    even, odd = bufs[1:]

    @frames_before
    def _(there):
        if there:
            load_frame(frame.at[0], up[0], down[0], gain, bufs, edges)
        for s, n in chunks(rows, cells, residual):
            total = acc_first[s : s + n]
            if there:
                total = total + taps(even, odd, k0, s, n, cells)
            if residual:
                result.finish(total, bias, s, n, cells)
            else:
                r, value = finish(total, bias, s, n, cells)
                out[0, r] = value.astype(BF16)

    if residual:
        result.wait(chunks(rows, cells, True))
    else:
        edges_out[0] = out[0, 0]
        edges_out[1] = out[0, rows - 1]
        inner[0] = out[0, 1 : rows - 1]


def whole(shape):
    return pl.BlockSpec(tuple(shape), lambda i: (0,) * len(shape))


def part(shape, index):
    return pl.BlockSpec((1, *shape[1:]), lambda i: (index,) + (0,) * (len(shape) - 1))


def call(body, name, units, out_specs, out_shape, args, aliases=None, extra=()):
    rows, cells, channels = call.block
    flat = (rows + 2) * cells
    arrays = [a for a, _ in args]
    flops = units * 2 * rows * cells * 9 * channels * channels
    return pl.pallas_call(
        body,
        grid=(1,),
        in_specs=[s for _, s in args],
        out_specs=out_specs,
        out_shape=out_shape,
        scratch_shapes=[
            pltpu.VMEM((3, flat, channels), F32),
            pltpu.VMEM((flat, 3 * channels), BF16),
            pltpu.VMEM((flat - 2 * cells, 3 * channels), BF16),
            *extra,
        ],
        input_output_aliases=aliases or {},
        compiler_params=pltpu.CompilerParams(vmem_limit_bytes=VMEM_LIMIT),
        cost_estimate=pl.CostEstimate(
            flops=flops, bytes_accessed=units * 2**21, transcendentals=2 * flat * channels
        ),
        name=name,
    )(*arrays)


def exchange_rows(inward, outward):
    bands = lax.axis_size("height")
    pairs = [(i, i ^ 1) for i in range(bands)]
    others = [(i, (i + (1 if i % 2 else -1)) % bands) for i in range(bands)]
    outward = lax.ppermute(outward, "height", others)
    return lax.ppermute(inward, "height", pairs), outward


def w(array):
    return array, whole(array.shape)


def shift(array, closed=True):
    route = ring("tm", 1)
    return lax.ppermute(array, "tm", route if closed else route[:-1])


def shapes():
    rows, cells, channels = call.block
    acc = jax.ShapeDtypeStruct((rows * cells, channels), F32)
    frame = jax.ShapeDtypeStruct((1, rows, cells, channels), BF16)
    inner = jax.ShapeDtypeStruct((1, rows - 2, cells, channels), BF16)
    edge = jax.ShapeDtypeStruct((2, cells, channels), BF16)
    return acc, frame, inner, edge


def own(last, first, up, down, gain, k, token):
    acc = shapes()[0]
    args = [last, first, w(up), w(down), gain, k[1], k[2], (token, pl.BlockSpec(memory_space=pl.ANY))]
    return call(own_kernel, "own", 3, [whole(acc.shape)] * 2, [acc, acc], args)


def own_apart(last, first, up, down, gain, k, early, late):
    acc = shapes()[0]
    up, down = pairs(up, 1), pairs(down, 1)
    args = [last, up[1], down[1], gain, k[2], (early, pl.BlockSpec(memory_space=pl.ANY))]
    acc_last = call(own_last_kernel, "last", 1, [whole(acc.shape)], [acc], args)[0]
    args = [first, up[0], down[0], gain, k[1], k[2], w(acc_last), (late, pl.BlockSpec(memory_space=pl.ANY))]
    return call(own_first_kernel, "first", 2, [whole(acc.shape)] * 2, [acc, acc], args)


def inner_rows(latents, token):
    rows = latents.shape[1]
    inner = shapes()[2]

    def copy(last, first, _, last_out, first_out):
        last_out[...] = last[:, 1 : rows - 1]
        first_out[...] = first[:, 1 : rows - 1]

    return pl.pallas_call(
        copy,
        grid=(1,),
        in_specs=[part(latents.shape, 1), part(latents.shape, 0), pl.BlockSpec(memory_space=pl.ANY)],
        out_specs=[whole(inner.shape)] * 2,
        out_shape=[inner] * 2,
        compiler_params=pltpu.CompilerParams(vmem_limit_bytes=6 * 2**20),
        name="inner",
    )(latents, latents, token)


def rows_after(token, *sources, plain=False):
    count = len(sources)

    def copy(*refs):
        inward, outward, *rows = refs[2 * count + (token is not None) :]
        lower = lax.axis_index("height") % 2 == 0
        for n in range(count):
            top, bottom = (ref.reshape(inward.shape[1:])[...] for ref in refs[2 * n : 2 * n + 2])
            inward[n] = jnp.where(lower, bottom, top)
            outward[n] = jnp.where(lower, top, bottom)
            if plain:
                rows[0][2 * n] = top
                rows[0][2 * n + 1] = bottom

    args = []
    for array, *places in sources:
        for place in places:
            block = (1,) * len(place) + array.shape[len(place) :]
            tail = (0,) * (array.ndim - len(place))
            args.append((array, pl.BlockSpec(block, lambda i, p=place, t=tail: (*p, *t))))
    if token is not None:
        args.append((token, pl.BlockSpec(memory_space=pl.ANY)))
    row = sources[0][0].shape[-2:]
    outs = [jax.ShapeDtypeStruct((n, *row), BF16) for n in [count] * 2 + [2 * count] * plain]
    return pl.pallas_call(
        copy,
        grid=(1,),
        in_specs=[spec for _, spec in args],
        out_specs=[whole(o.shape) for o in outs],
        out_shape=outs,
        compiler_params=pltpu.CompilerParams(vmem_limit_bytes=4 * 2**20),
        name="edges",
    )(*[array for array, _ in args])


def pairs(array, size):
    block = (size, *array.shape[1:])
    return [
        (array, pl.BlockSpec(block, lambda i, n=n: (n,) + (0,) * (len(block) - 1)))
        for n in range(array.shape[0] // size)
    ]


def first_section(latents, gain, kernel, bias):
    bottom = latents.shape[1] - 1
    acc, frame, inner, edge = shapes()
    k = [(kernel, part(kernel.shape, i)) for i in range(3)]
    first, last = ((latents, part(latents.shape, i)) for i in range(2))
    sources = [(latents, (i, 0), (i, bottom)) for i in range(2)]
    edges = latents[:, ::bottom].reshape(4, *latents.shape[2:])
    sides = rows_after(None, *sources)
    edges = shift(edges)
    up, down = exchange_rows(*sides)
    inner_last, inner_first = inner_rows(latents, sides[0])
    before, earliest = shift(inner_last), shift(inner_first, False)

    sides = rows_after(up, (edges, (2,), (3,)), (edges, (0,), (1,)))
    acc_first, acc_last = own(last, first, up, down, gain, k, sides[0])
    up, down = (pairs(a, 1) for a in exchange_rows(*sides))
    edges = pairs(edges, 2)
    outs = [frame, acc]
    y_last, acc_first = call(
        functools.partial(before_kernel, False),
        "before",
        2,
        [whole(o.shape) for o in outs],
        outs,
        [w(before), edges[1], up[0], down[0], gain, k[0], k[1], bias, w(acc_first), w(acc_last)],
    )
    outs = [frame, inner, edge]
    y_first, inner_first, edge_first = call(
        functools.partial(earliest_kernel, False),
        "earliest",
        1,
        [whole(o.shape) for o in outs],
        outs,
        [w(earliest), edges[0], up[1], down[1], gain, k[0], bias, w(acc_first)],
    )
    return y_last, y_first, inner_first, edge_first


def second_section(results, latents, gain, kernel, bias):
    y_last, y_first, inner_first, edge_first = results
    bottom = latents.shape[1] - 1
    acc = shapes()[0]
    k = [(kernel, part(kernel.shape, i)) for i in range(3)]
    before = shift(y_last)
    edges = shift(edge_first)
    earliest = shift(inner_first)
    up, down = exchange_rows(
        *rows_after(edge_first, (y_first, (0, 0), (0, bottom)), (y_last, (0, 0), (0, bottom)))
    )
    sides = rows_after(up, (before, (0, 0), (0, bottom)))
    acc_first, acc_last = own_apart(w(y_last), w(y_first), up, down, gain, k, up, sides[0])

    out = jax.ShapeDtypeStruct(latents.shape, BF16)
    anywhere = pl.BlockSpec(memory_space=pl.ANY)
    extra = [pltpu.VMEM(latents.shape[1:], BF16), pltpu.SemaphoreType.DMA((len(chunks(*latents.shape[1:3], True)),))]
    args = [w(before), *map(w, exchange_rows(*sides)), gain, k[0], k[1], bias, w(acc_first), w(acc_last)]
    args.append((latents, part(latents.shape, 1)))
    half, acc_first = call(
        functools.partial(before_kernel, True),
        "before",
        2,
        [anywhere, whole(acc.shape)],
        [out, acc],
        args,
        extra=extra,
    )
    sides = rows_after(acc_last, (edges, (0,), (1,)))
    args = [w(earliest), w(edges), *map(w, exchange_rows(*sides)), gain, k[0], bias, w(acc_first)]
    args += [(latents, part(latents.shape, 0)), (half, anywhere)]
    body = functools.partial(earliest_kernel, True)
    return call(body, "earliest", 1, anywhere, out, args, {len(args) - 1: 0}, extra)


def per_device(
    latents, first_gain, first_kernel, first_bias, second_gain, second_kernel, second_bias
):
    frames, rows, cells, channels = latents.shape
    call.block = (rows, cells, channels)

    def columns(kernel):
        return kernel.reshape(3, 3, 3 * channels, channels)

    first_gain, first_bias, second_gain, second_bias = map(w, (first_gain, first_bias, second_gain, second_bias))
    results = first_section(latents, first_gain, columns(first_kernel), first_bias)
    return second_section(results, latents, second_gain, columns(second_kernel), second_bias)


def solution(mesh):
    return jax.shard_map(
        per_device,
        mesh=mesh,
        in_specs=(P("tm", "height", None, None), P(), P(), P(), P(), P(), P()),
        out_specs=P("tm", "height", None, None),
        check_vma=False,
    )
```

```python
import functools

import jax
import jax.numpy as jnp
from jax import lax
from jax.experimental import pallas as pl
from jax.experimental.pallas import tpu as pltpu
from jax.sharding import PartitionSpec as P

EPSILON = 1e-06
BF16, F32 = jnp.bfloat16, jnp.float32
VMEM_LIMIT = 26 * 2**20


def ring(axis, step):
    peers = lax.axis_size(axis)
    return [(i, (i + step) % peers) for i in range(peers)]


def activate(row, gain, mask):
    cells = row.shape[0]
    values = row.astype(F32)
    mean_power = jnp.mean(values * values, axis=-1, keepdims=True)
    normed = values * lax.rsqrt(mean_power + EPSILON) * gain
    act = normed / (1.0 + jnp.exp(-normed))
    if mask is not None:
        act = act * mask
    cell = lax.broadcasted_iota(jnp.int32, act.shape, 0)
    left = jnp.where(cell == 0, 0.0, pltpu.roll(act, 1, 0))
    right = jnp.where(cell == cells - 1, 0.0, pltpu.roll(act, cells - 1, 0))
    return left, act, right


def activate_rows(get_row, gain, shifts, rows, cells):
    for r in range(rows):
        values, mask = get_row(r)
        here = slice(r * cells, (r + 1) * cells)
        if values is None:
            shifts[:, here, :] = jnp.zeros((3, cells, shifts.shape[-1]), F32)
            continue
        for l, value in enumerate(activate(values, gain, mask)):
            shifts[l, here, :] = value


def pack(shifts, even, odd, rows, cells):
    channels = shifts.shape[-1]
    pair = 2 * cells
    for buf, first, count in ((even, 0, rows // 2), (odd, cells, rows // 2 - 1)):
        for k in range(count):
            for l in range(3):
                buf[k * pair : (k + 1) * pair, l * channels : (l + 1) * channels] = shifts[
                    l, first + k * pair : first + (k + 1) * pair, :
                ].astype(BF16)


def taps(even, odd, kernel, start, length, cells):
    dot = functools.partial(jnp.dot, preferred_element_type=F32)
    lower = 2 * cells + start
    return (
        dot(even[start : start + length], kernel[0, 0])
        + dot(odd[start : start + length], kernel[0, 1])
        + dot(even[lower : lower + length], kernel[0, 2])
    )


def masks():
    row_id, rows = lax.axis_index("height"), lax.axis_size("height")
    above = (row_id > 0).astype(F32)
    below = (row_id < rows - 1).astype(F32)
    return above, below


def load_frame(frame, inward, outward, gain, bufs, edges=None):
    shifts, even, odd = bufs
    rows, cells = frame.shape[0], frame.shape[1]
    if edges is not None:
        rows += 2
    above, below = masks()

    lower = lax.axis_index("height") % 2 == 0

    def get_row(r):
        if inward is None and r in (0, rows + 1):
            return None, None
        if r == 0:
            return jnp.where(lower, outward, inward), above
        if r == rows + 1:
            return jnp.where(lower, inward, outward), below
        if edges is None:
            return frame[r - 1], None
        if r in (1, rows):
            return edges[0 if r == 1 else 1], None
        return frame[r - 2], None

    activate_rows(get_row, gain[...].astype(F32)[None], shifts, rows + 2, cells)
    pack(shifts, even, odd, rows + 2, cells)


def chunks(rows, cells, fine=False):
    step = 4 * cells if rows % 4 == 0 and not fine else 2 * cells
    return [(s, step) for s in range(0, rows * cells, step)]


def own_kernel(last, first, up, down, gain, k1, k2, _, acc_first, acc_last, *bufs):
    rows, cells = last.shape[1], last.shape[2]
    even, odd = bufs[1:]
    load_frame(last.at[0], up[1], down[1], gain, bufs)
    for s, n in chunks(rows, cells):
        acc_last[s : s + n] = taps(even, odd, k2, s, n, cells)
    load_frame(first.at[0], up[0], down[0], gain, bufs)
    for s, n in chunks(rows, cells):
        acc_last[s : s + n] += taps(even, odd, k1, s, n, cells)
        acc_first[s : s + n] = taps(even, odd, k2, s, n, cells)


def own_last_kernel(last, gain, k2, acc_last, *bufs):
    rows, cells = last.shape[1], last.shape[2]
    even, odd = bufs[1:]
    load_frame(last.at[0], None, None, gain, bufs)
    for s, n in chunks(rows, cells):
        acc_last[s : s + n] = taps(even, odd, k2, s, n, cells)


def own_first_kernel(first, up, down, last_up, last_down, gain, k1, k2, acc_in, _, acc_first, acc_last, *bufs):
    rows, cells = first.shape[1], first.shape[2]
    even, odd = bufs[1:]
    load_frame(first.at[0], up[0], down[0], gain, bufs)
    for s, n in chunks(rows, cells):
        acc_last[s : s + n] = acc_in[s : s + n] + taps(even, odd, k1, s, n, cells)
        acc_first[s : s + n] = taps(even, odd, k2, s, n, cells)
    lower = lax.axis_index("height") % 2 == 0
    weight = gain[...].astype(F32)[None]
    for edge, mask in enumerate(masks()):
        pair = (last_down[0], last_up[0]) if edge == 0 else (last_up[0], last_down[0])
        row = jnp.concatenate(activate(jnp.where(lower, *pair), weight, mask), axis=1).astype(BF16)
        here = slice(0, cells) if edge == 0 else slice((rows - 1) * cells, rows * cells)
        acc_last[here] += jnp.dot(row, k2[0, 2 * edge], preferred_element_type=F32)


def finish(total, bias, s, n, cells):
    value = (total + bias[...].astype(F32)[None]).reshape(n // cells, cells, -1)
    return slice(s // cells, (s + n) // cells), value


class Result:
    def __init__(self, latents, out, frame, rows, sems):
        self.residual, self.out, self.frame, self.rows, self.sems = latents.at[0], out, frame, rows, sems

    def copy(self, s, n, cells):
        r = pl.ds(s // cells, n // cells)
        return pltpu.make_async_copy(
            self.rows.at[r], self.out.at[self.frame, r], self.sems.at[s // n]
        )

    def finish(self, total, bias, s, n, cells):
        r, value = finish(total, bias, s, n, cells)
        self.rows[r] = (self.residual[r].astype(F32) + value).astype(BF16)
        self.copy(s, n, cells).start()

    def wait(self, parts):
        for s, n in parts:
            self.copy(s, n, self.rows.shape[1]).wait()


def frames_before(body):
    first = lax.axis_index("tm") == 0
    pl.when(first)(lambda: body(False))
    pl.when(jnp.logical_not(first))(lambda: body(True))


def before_kernel(residual, *refs):
    if residual:
        frame, up, down, gain, k0, k1, bias, acc_first, acc_last, latents, out, acc_out, *bufs, new, sems = refs
        frame, edges = frame.at[0], None
        result = Result(latents, out, 1, new, sems)
    else:
        frame, edges, up, down, gain, k0, k1, bias, acc_first, acc_last, out, acc_out, *bufs = refs
        frame = frame.at[0]
    cells = up.shape[1]
    rows = acc_first.shape[0] // cells
    even, odd = bufs[1:]

    @frames_before
    def _(there):
        if there:
            load_frame(frame, up[0], down[0], gain, bufs, edges)
        for s, n in chunks(rows, cells):
            total = acc_last[s : s + n]
            if there:
                total = total + taps(even, odd, k0, s, n, cells)
            if residual:
                result.finish(total, bias, s, n, cells)
            else:
                r, value = finish(total, bias, s, n, cells)
                out[0, r] = value.astype(BF16)
        for s, n in chunks(rows, cells):
            total = acc_first[s : s + n]
            if there:
                total = total + taps(even, odd, k1, s, n, cells)
            acc_out[s : s + n] = total

    if residual:
        result.wait(chunks(rows, cells))


def earliest_kernel(frame, edges, up, down, gain, k0, bias, acc_first, _, out, *bufs):
    cells = up.shape[1]
    rows = acc_first.shape[0] // cells
    even, odd = bufs[1:]

    @frames_before
    def _(there):
        if there:
            load_frame(frame.at[0], up[0], down[0], gain, bufs, edges)
        for s, n in chunks(rows, cells):
            total = acc_first[s : s + n]
            if there:
                total = total + taps(even, odd, k0, s, n, cells)
            r, value = finish(total, bias, s, n, cells)
            out[0, r] = value.astype(BF16)


def ahead_kernel(frame, gain, k0, inner, edge_acc, *bufs):
    rows, cells = frame.shape[1], frame.shape[2]
    even, odd = bufs[1:]
    load_frame(frame.at[0], None, None, gain, bufs)
    for s, n in chunks(rows, cells):
        total = taps(even, odd, k0, s, n, cells)
        value = total.reshape(n // cells, cells, -1).astype(BF16)
        first = s // cells
        low, high = max(first, 1), min(first + n // cells, rows - 1)
        inner[0, low - 1 : high - 1] = value[low - first : high - first]
        if s == 0:
            edge_acc[0] = total[:cells]
        if s + n == rows * cells:
            edge_acc[1] = total[n - cells :]


def edges_kernel(inward, outward, gain, k0, edge_acc, _, edges, columns):
    lower = lax.axis_index("height") % 2 == 0
    weight = gain[...].astype(F32)[None]
    for edge, mask in enumerate(masks()):
        pair = (outward[0], inward[0]) if edge == 0 else (inward[0], outward[0])
        for l, value in enumerate(activate(jnp.where(lower, *pair), weight, mask)):
            size = value.shape[-1]
            columns[:, l * size : (l + 1) * size] = value.astype(BF16)
        add = jnp.dot(columns[...], k0[0, 2 * edge], preferred_element_type=F32)
        edges[edge] = (edge_acc[edge] + add).astype(BF16)


def received(value):
    return jnp.where(lax.axis_index("tm") > 0, value.astype(F32), 0.0)


def sum_kernel(inner, edges, acc_first, bias, residual, _, out, rows, sems):
    count, cells = residual.shape[1], residual.shape[2]
    copies = []
    for n in range(2):
        low, high = n * (count // 2), (n + 1) * (count // 2)
        for r in range(low, high):
            ahead = edges[0 if r == 0 else 1] if r in (0, count - 1) else inner[0, r - 1]
            total = acc_first[r * cells : (r + 1) * cells] + bias[...].astype(F32)[None] + received(ahead)
            rows[r] = (residual[0, r].astype(F32) + total).astype(BF16)
        half = pl.ds(low, count // 2)
        copies.append(pltpu.make_async_copy(rows.at[half], out.at[0, half], sems.at[n]))
        copies[-1].start()
    for copy in copies:
        copy.wait()


def whole(shape):
    return pl.BlockSpec(tuple(shape), lambda i: (0,) * len(shape))


def part(shape, index):
    return pl.BlockSpec((1, *shape[1:]), lambda i: (index,) + (0,) * (len(shape) - 1))


def call(body, name, units, out_specs, out_shape, args, aliases=None, scratch=None, limit=VMEM_LIMIT):
    rows, cells, channels = call.block
    flat = (rows + 2) * cells
    arrays = [a for a, _ in args]
    flops = int(units * 2 * rows * cells * 9 * channels * channels)
    return pl.pallas_call(
        body,
        grid=(1,),
        in_specs=[s for _, s in args],
        out_specs=out_specs,
        out_shape=out_shape,
        scratch_shapes=scratch
        or [
            pltpu.VMEM((3, flat, channels), F32),
            pltpu.VMEM((flat, 3 * channels), BF16),
            pltpu.VMEM((flat - 2 * cells, 3 * channels), BF16),
        ],
        input_output_aliases=aliases or {},
        compiler_params=pltpu.CompilerParams(vmem_limit_bytes=limit),
        cost_estimate=pl.CostEstimate(
            flops=flops, bytes_accessed=int(units * 2**21), transcendentals=2 * flat * channels
        ),
        name=name,
    )(*arrays)


def exchange_rows(inward, outward):
    bands = lax.axis_size("height")
    pairs = [(i, i ^ 1) for i in range(bands)]
    others = [(i, (i + (1 if i % 2 else -1)) % bands) for i in range(bands)]
    outward = lax.ppermute(outward, "height", others)
    return lax.ppermute(inward, "height", pairs), outward


def w(array):
    return array, whole(array.shape)


def shift(array, closed=True):
    route = ring("tm", 1)
    return lax.ppermute(array, "tm", route if closed else route[:-1])


def rest(array):
    return array, pl.BlockSpec(memory_space=pl.ANY)


def shapes():
    rows, cells, channels = call.block
    acc = jax.ShapeDtypeStruct((rows * cells, channels), F32)
    frame = jax.ShapeDtypeStruct((1, rows, cells, channels), BF16)
    inner = jax.ShapeDtypeStruct((1, rows - 2, cells, channels), BF16)
    edge = jax.ShapeDtypeStruct((2, cells, channels), BF16)
    return acc, frame, inner, edge


def own(last, first, up, down, gain, k, token):
    acc = shapes()[0]
    args = [last, first, w(up), w(down), gain, k[1], k[2], (token, pl.BlockSpec(memory_space=pl.ANY))]
    return call(own_kernel, "own", 3, [whole(acc.shape)] * 2, [acc, acc], args)


def own_last(last, gain, k):
    acc = shapes()[0]
    return call(own_last_kernel, "last", 1, [whole(acc.shape)], [acc], [last, gain, k[2]])[0]


def own_first(first, up, down, gain, k, acc_last, token):
    acc = shapes()[0]
    up, down = pairs(up, 1), pairs(down, 1)
    args = [first, up[0], down[0], up[1], down[1], gain, k[1], k[2], w(acc_last), rest(token)]
    return call(own_first_kernel, "first", 2, [whole(acc.shape)] * 2, [acc, acc], args)


def inner_rows(latents, token):
    rows = latents.shape[1]
    inner = shapes()[2]

    def copy(last, first, _, last_out, first_out):
        last_out[...] = last[:, 1 : rows - 1]
        first_out[...] = first[:, 1 : rows - 1]

    return pl.pallas_call(
        copy,
        grid=(1,),
        in_specs=[part(latents.shape, 1), part(latents.shape, 0), pl.BlockSpec(memory_space=pl.ANY)],
        out_specs=[whole(inner.shape)] * 2,
        out_shape=[inner] * 2,
        compiler_params=pltpu.CompilerParams(vmem_limit_bytes=6 * 2**20),
        name="inner",
    )(latents, latents, token)


def rows_after(token, *sources, plain=False):
    count = len(sources)

    def copy(*refs):
        inward, outward, *rows = refs[2 * count + (token is not None) :]
        lower = lax.axis_index("height") % 2 == 0
        for n in range(count):
            top, bottom = (ref.reshape(inward.shape[1:])[...] for ref in refs[2 * n : 2 * n + 2])
            inward[n] = jnp.where(lower, bottom, top)
            outward[n] = jnp.where(lower, top, bottom)
            if plain:
                rows[0][2 * n] = top
                rows[0][2 * n + 1] = bottom

    args = []
    for array, *places in sources:
        for place in places:
            block = (1,) * len(place) + array.shape[len(place) :]
            tail = (0,) * (array.ndim - len(place))
            args.append((array, pl.BlockSpec(block, lambda i, p=place, t=tail: (*p, *t))))
    if token is not None:
        args.append((token, pl.BlockSpec(memory_space=pl.ANY)))
    row = sources[0][0].shape[-2:]
    outs = [jax.ShapeDtypeStruct((n, *row), BF16) for n in [count] * 2 + [2 * count] * plain]
    return pl.pallas_call(
        copy,
        grid=(1,),
        in_specs=[spec for _, spec in args],
        out_specs=[whole(o.shape) for o in outs],
        out_shape=outs,
        compiler_params=pltpu.CompilerParams(vmem_limit_bytes=4 * 2**20),
        name="edges",
    )(*[array for array, _ in args])


def pairs(array, size):
    block = (size, *array.shape[1:])
    return [
        (array, pl.BlockSpec(block, lambda i, n=n: (n,) + (0,) * (len(block) - 1)))
        for n in range(array.shape[0] // size)
    ]


def first_section(latents, gain, kernel, bias, ahead):
    bottom = latents.shape[1] - 1
    acc, frame, inner, edge = shapes()
    k = [(kernel, part(kernel.shape, i)) for i in range(3)]
    first, last = ((latents, part(latents.shape, i)) for i in range(2))
    sources = [(latents, (i, 0), (i, bottom)) for i in range(2)]
    edges = latents[:, ::bottom].reshape(4, *latents.shape[2:])
    sides = rows_after(None, *sources)
    edges = shift(edges)
    up, down = exchange_rows(*sides)
    inner_last, inner_first = inner_rows(latents, sides[0])
    before, earliest = shift(inner_last), shift(inner_first, False)

    sides = rows_after(up, (edges, (2,), (3,)), (edges, (0,), (1,)))
    acc_first, acc_last = own(last, first, up, down, gain, k, sides[0])
    up, down = (pairs(a, 1) for a in exchange_rows(*sides))
    edges = pairs(edges, 2)
    outs = [frame, acc]
    y_last, acc_first = call(
        functools.partial(before_kernel, False),
        "before",
        2,
        [whole(o.shape) for o in outs],
        outs,
        [w(before), edges[1], up[0], down[0], gain, k[0], k[1], bias, w(acc_first), w(acc_last)],
    )
    second_last = ahead(y_last)
    outs = [frame]
    (y_first,) = call(
        earliest_kernel,
        "earliest",
        1,
        [whole(o.shape) for o in outs],
        outs,
        [w(earliest), edges[0], up[1], down[1], gain, k[0], bias, w(acc_first), rest(second_last)],
    )
    return y_last, y_first, second_last


def second_section(results, latents, gain, kernel, bias):
    y_last, y_first, acc_last = results
    rows, cells, channels = latents.shape[1:]
    bottom = rows - 1
    acc, _, inner, edge = shapes()
    k = [(kernel, part(kernel.shape, i)) for i in range(3)]
    before = shift(y_last)
    frames = [(y, (0, 0), (0, bottom)) for y in (y_first, y_last)]
    up, down = exchange_rows(*rows_after(None, *frames))
    outs = [inner, jax.ShapeDtypeStruct(edge.shape, F32)]
    inner_ahead, edge_acc = call(
        ahead_kernel, "ahead", 1, [whole(o.shape) for o in outs], outs, [w(y_first), gain, k[0]]
    )
    inner_ahead = shift(inner_ahead)
    args = [pairs(up, 1)[0], pairs(down, 1)[0], gain, k[0], w(edge_acc), rest(acc_last)]
    columns = [pltpu.VMEM((cells, 3 * channels), BF16)]
    (edges_ahead,) = call(edges_kernel, "ends", 0, [whole(edge.shape)], [edge], args, scratch=columns)
    edges_ahead = shift(edges_ahead, False)
    sides = rows_after(up, (before, (0, 0), (0, bottom)))
    acc_first, acc_last = own_first(w(y_first), up, down, gain, k, acc_last, sides[0])

    out = jax.ShapeDtypeStruct(latents.shape, BF16)
    anywhere = pl.BlockSpec(memory_space=pl.ANY)
    extra = [pltpu.VMEM(latents.shape[1:], BF16), pltpu.SemaphoreType.DMA((2,))]
    flat = (rows + 2) * cells
    scratch = [
        pltpu.VMEM((3, flat, channels), F32),
        pltpu.VMEM((flat, 3 * channels), BF16),
        pltpu.VMEM((flat - 2 * cells, 3 * channels), BF16),
    ]
    args = [w(before), *map(w, exchange_rows(*sides)), gain, k[0], k[1], bias, w(acc_first), w(acc_last)]
    args.append((latents, part(latents.shape, 1)))
    half, acc_first = call(
        functools.partial(before_kernel, True),
        "before",
        2,
        [anywhere, whole(acc.shape)],
        [out, acc],
        args,
        scratch=scratch + extra,
    )
    args = [w(inner_ahead), w(edges_ahead), w(acc_first), bias, (latents, part(latents.shape, 0)), rest(half)]
    return call(sum_kernel, "sum", 0, anywhere, out, args, {len(args) - 1: 0}, extra, 12 * 2**20)


def per_device(
    latents, first_gain, first_kernel, first_bias, second_gain, second_kernel, second_bias
):
    frames, rows, cells, channels = latents.shape
    call.block = (rows, cells, channels)

    def columns(kernel):
        return kernel.reshape(3, 3, 3 * channels, channels)

    first_gain, first_bias, second_gain, second_bias = map(w, (first_gain, first_bias, second_gain, second_bias))
    second_kernel = columns(second_kernel)
    k = [(second_kernel, part(second_kernel.shape, i)) for i in range(3)]

    def ahead(y_last):
        return own_last(w(y_last), second_gain, k)

    results = first_section(latents, first_gain, columns(first_kernel), first_bias, ahead)
    return second_section(results, latents, second_gain, second_kernel, second_bias)


def solution(mesh):
    return jax.shard_map(
        per_device,
        mesh=mesh,
        in_specs=(P("tm", "height", None, None), P(), P(), P(), P(), P(), P()),
        out_specs=P("tm", "height", None, None),
        check_vma=False,
    )
```

```python
import functools

import jax
import jax.numpy as jnp
from jax import lax
from jax.experimental import pallas as pl
from jax.experimental.pallas import tpu as pltpu
from jax.sharding import PartitionSpec as P

EPSILON = 1e-06
BF16, F32 = jnp.bfloat16, jnp.float32
VMEM_LIMIT = 26 * 2**20


def ring(axis, step):
    peers = lax.axis_size(axis)
    return [(i, (i + step) % peers) for i in range(peers)]


def activate(row, gain, mask):
    cells = row.shape[0]
    values = row.astype(F32)
    mean_power = jnp.mean(values * values, axis=-1, keepdims=True)
    normed = values * lax.rsqrt(mean_power + EPSILON) * gain
    act = normed / (1.0 + jnp.exp(-normed))
    if mask is not None:
        act = act * mask
    cell = lax.broadcasted_iota(jnp.int32, act.shape, 0)
    left = jnp.where(cell == 0, 0.0, pltpu.roll(act, 1, 0))
    right = jnp.where(cell == cells - 1, 0.0, pltpu.roll(act, cells - 1, 0))
    return left, act, right


def activate_rows(get_row, gain, shifts, rows, cells):
    for r in range(rows):
        values, mask = get_row(r)
        here = slice(r * cells, (r + 1) * cells)
        if values is None:
            shifts[:, here, :] = jnp.zeros((3, cells, shifts.shape[-1]), F32)
            continue
        for l, value in enumerate(activate(values, gain, mask)):
            shifts[l, here, :] = value


def pack(shifts, even, odd, rows, cells):
    channels = shifts.shape[-1]
    pair = 2 * cells
    for buf, first, count in ((even, 0, rows // 2), (odd, cells, rows // 2 - 1)):
        for k in range(count):
            for l in range(3):
                buf[k * pair : (k + 1) * pair, l * channels : (l + 1) * channels] = shifts[
                    l, first + k * pair : first + (k + 1) * pair, :
                ].astype(BF16)


def taps(even, odd, kernel, start, length, cells):
    dot = functools.partial(jnp.dot, preferred_element_type=F32)
    lower = 2 * cells + start
    return (
        dot(even[start : start + length], kernel[0, 0])
        + dot(odd[start : start + length], kernel[0, 1])
        + dot(even[lower : lower + length], kernel[0, 2])
    )


def masks():
    row_id, rows = lax.axis_index("height"), lax.axis_size("height")
    above = (row_id > 0).astype(F32)
    below = (row_id < rows - 1).astype(F32)
    return above, below


def load_frame(frame, inward, outward, gain, bufs, edges=None):
    shifts, even, odd = bufs
    rows, cells = frame.shape[0], frame.shape[1]
    if edges is not None:
        rows += 2
    above, below = masks()

    lower = lax.axis_index("height") % 2 == 0

    def get_row(r):
        if inward is None and r in (0, rows + 1):
            return None, None
        if r == 0:
            return jnp.where(lower, outward, inward), above
        if r == rows + 1:
            return jnp.where(lower, inward, outward), below
        if edges is None:
            return frame[r - 1], None
        if r in (1, rows):
            return edges[0 if r == 1 else 1], None
        return frame[r - 2], None

    activate_rows(get_row, gain[...].astype(F32)[None], shifts, rows + 2, cells)
    pack(shifts, even, odd, rows + 2, cells)


def chunks(rows, cells, fine=False):
    step = 4 * cells if rows % 4 == 0 and not fine else 2 * cells
    return [(s, step) for s in range(0, rows * cells, step)]


def own_kernel(last, first, up, down, gain, k1, k2, _, acc_first, acc_last, *bufs):
    rows, cells = last.shape[1], last.shape[2]
    even, odd = bufs[1:]
    load_frame(last.at[0], up[1], down[1], gain, bufs)
    for s, n in chunks(rows, cells):
        acc_last[s : s + n] = taps(even, odd, k2, s, n, cells)
    load_frame(first.at[0], up[0], down[0], gain, bufs)
    for s, n in chunks(rows, cells):
        acc_last[s : s + n] += taps(even, odd, k1, s, n, cells)
        acc_first[s : s + n] = taps(even, odd, k2, s, n, cells)


def own_last_kernel(last, gain, k2, acc_last, *bufs):
    rows, cells = last.shape[1], last.shape[2]
    even, odd = bufs[1:]
    load_frame(last.at[0], None, None, gain, bufs)
    for s, n in chunks(rows, cells):
        acc_last[s : s + n] = taps(even, odd, k2, s, n, cells)


def own_first_kernel(first, up, down, last_up, last_down, gain, k1, k2, bias, residual, acc_in, _, acc_first, acc_last, *bufs):
    rows, cells = first.shape[1], first.shape[2]
    even, odd = bufs[1:]
    load_frame(first.at[0], up[0], down[0], gain, bufs)
    for s, n in chunks(rows, cells):
        acc_last[s : s + n] = acc_in[s : s + n] + taps(even, odd, k1, s, n, cells)
        share = residual[0, s // cells : (s + n) // cells].astype(F32).reshape(n, -1) + bias[...].astype(F32)[None]
        acc_first[s : s + n] = share + taps(even, odd, k2, s, n, cells)
    lower = lax.axis_index("height") % 2 == 0
    weight = gain[...].astype(F32)[None]
    for edge, mask in enumerate(masks()):
        pair = (last_down[0], last_up[0]) if edge == 0 else (last_up[0], last_down[0])
        row = jnp.concatenate(activate(jnp.where(lower, *pair), weight, mask), axis=1).astype(BF16)
        here = slice(0, cells) if edge == 0 else slice((rows - 1) * cells, rows * cells)
        acc_last[here] += jnp.dot(row, k2[0, 2 * edge], preferred_element_type=F32)


def finish(total, bias, s, n, cells):
    value = (total + bias[...].astype(F32)[None]).reshape(n // cells, cells, -1)
    return slice(s // cells, (s + n) // cells), value


class Result:
    def __init__(self, latents, out, frame, rows, sems):
        self.residual, self.out, self.frame, self.rows, self.sems = latents.at[0], out, frame, rows, sems

    def copy(self, s, n, cells):
        r = pl.ds(s // cells, n // cells)
        return pltpu.make_async_copy(
            self.rows.at[r], self.out.at[self.frame, r], self.sems.at[s // n]
        )

    def finish(self, total, bias, s, n, cells):
        r, value = finish(total, bias, s, n, cells)
        self.rows[r] = (self.residual[r].astype(F32) + value).astype(BF16)
        self.copy(s, n, cells).start()

    def wait(self, parts):
        for s, n in parts:
            self.copy(s, n, self.rows.shape[1]).wait()


def frames_before(body):
    first = lax.axis_index("tm") == 0
    pl.when(first)(lambda: body(False))
    pl.when(jnp.logical_not(first))(lambda: body(True))


def before_kernel(residual, *refs):
    if residual:
        frame, up, down, gain, k0, k1, bias, acc_first, acc_last, latents, out, acc_out, *bufs, new, sems = refs
        frame, edges = frame.at[0], None
        result = Result(latents, out, 1, new, sems)
    else:
        frame, edges, up, down, gain, k0, k1, bias, acc_first, acc_last, out, acc_out, *bufs = refs
        frame = frame.at[0]
    cells = up.shape[1]
    rows = acc_first.shape[0] // cells
    even, odd = bufs[1:]

    @frames_before
    def _(there):
        if there:
            load_frame(frame, up[0], down[0], gain, bufs, edges)
        for s, n in chunks(rows, cells):
            total = acc_last[s : s + n]
            if there:
                total = total + taps(even, odd, k0, s, n, cells)
            if residual:
                result.finish(total, bias, s, n, cells)
            else:
                r, value = finish(total, bias, s, n, cells)
                out[0, r] = value.astype(BF16)
        for s, n in chunks(rows, cells):
            total = acc_first[s : s + n]
            if there:
                total = total + taps(even, odd, k1, s, n, cells)
            acc_out[s : s + n] = total

    if residual:
        result.wait(chunks(rows, cells))


def earliest_kernel(frame, edges, up, down, gain, k0, bias, acc_first, _, out, *bufs):
    cells = up.shape[1]
    rows = acc_first.shape[0] // cells
    even, odd = bufs[1:]

    @frames_before
    def _(there):
        if there:
            load_frame(frame.at[0], up[0], down[0], gain, bufs, edges)
        for s, n in chunks(rows, cells):
            total = acc_first[s : s + n]
            if there:
                total = total + taps(even, odd, k0, s, n, cells)
            r, value = finish(total, bias, s, n, cells)
            out[0, r] = value.astype(BF16)


def ahead_kernel(frame, gain, k0, inner, edge_acc, *bufs):
    rows, cells = frame.shape[1], frame.shape[2]
    even, odd = bufs[1:]
    load_frame(frame.at[0], None, None, gain, bufs)
    for s, n in chunks(rows, cells):
        total = taps(even, odd, k0, s, n, cells)
        value = total.reshape(n // cells, cells, -1).astype(BF16)
        first = s // cells
        low, high = max(first, 1), min(first + n // cells, rows - 1)
        inner[0, low - 1 : high - 1] = value[low - first : high - first]
        if s == 0:
            edge_acc[0] = total[:cells]
        if s + n == rows * cells:
            edge_acc[1] = total[n - cells :]


def edges_kernel(inward, outward, gain, k0, edge_acc, _, edges, columns):
    lower = lax.axis_index("height") % 2 == 0
    weight = gain[...].astype(F32)[None]
    for edge, mask in enumerate(masks()):
        pair = (outward[0], inward[0]) if edge == 0 else (inward[0], outward[0])
        for l, value in enumerate(activate(jnp.where(lower, *pair), weight, mask)):
            size = value.shape[-1]
            columns[:, l * size : (l + 1) * size] = value.astype(BF16)
        add = jnp.dot(columns[...], k0[0, 2 * edge], preferred_element_type=F32)
        edges[edge] = (edge_acc[edge] + add).astype(BF16)


def received(value):
    return jnp.where(lax.axis_index("tm") > 0, value.astype(F32), 0.0)


def sum_kernel(inner, edges, acc_first, _, out, rows, sems):
    count, cells = rows.shape[0], rows.shape[1]
    copies = []
    for n in range(2):
        low, high = n * (count // 2), (n + 1) * (count // 2)
        for r in range(low, high):
            ahead = edges[0 if r == 0 else 1] if r in (0, count - 1) else inner[0, r - 1]
            rows[r] = (acc_first[r * cells : (r + 1) * cells] + received(ahead)).astype(BF16)
        half = pl.ds(low, count // 2)
        copies.append(pltpu.make_async_copy(rows.at[half], out.at[0, half], sems.at[n]))
        copies[-1].start()
    for copy in copies:
        copy.wait()


def whole(shape):
    return pl.BlockSpec(tuple(shape), lambda i: (0,) * len(shape))


def part(shape, index):
    return pl.BlockSpec((1, *shape[1:]), lambda i: (index,) + (0,) * (len(shape) - 1))


def call(body, name, units, out_specs, out_shape, args, aliases=None, scratch=None, limit=VMEM_LIMIT):
    rows, cells, channels = call.block
    flat = (rows + 2) * cells
    arrays = [a for a, _ in args]
    flops = int(units * 2 * rows * cells * 9 * channels * channels)
    return pl.pallas_call(
        body,
        grid=(1,),
        in_specs=[s for _, s in args],
        out_specs=out_specs,
        out_shape=out_shape,
        scratch_shapes=scratch
        or [
            pltpu.VMEM((3, flat, channels), F32),
            pltpu.VMEM((flat, 3 * channels), BF16),
            pltpu.VMEM((flat - 2 * cells, 3 * channels), BF16),
        ],
        input_output_aliases=aliases or {},
        compiler_params=pltpu.CompilerParams(vmem_limit_bytes=limit),
        cost_estimate=pl.CostEstimate(
            flops=flops, bytes_accessed=int(units * 2**21), transcendentals=2 * flat * channels
        ),
        name=name,
    )(*arrays)


def exchange_rows(inward, outward):
    bands = lax.axis_size("height")
    pairs = [(i, i ^ 1) for i in range(bands)]
    others = [(i, (i + (1 if i % 2 else -1)) % bands) for i in range(bands)]
    outward = lax.ppermute(outward, "height", others)
    return lax.ppermute(inward, "height", pairs), outward


def w(array):
    return array, whole(array.shape)


def shift(array, closed=True):
    route = ring("tm", 1)
    return lax.ppermute(array, "tm", route if closed else route[:-1])


def rest(array):
    return array, pl.BlockSpec(memory_space=pl.ANY)


def shapes():
    rows, cells, channels = call.block
    acc = jax.ShapeDtypeStruct((rows * cells, channels), F32)
    frame = jax.ShapeDtypeStruct((1, rows, cells, channels), BF16)
    inner = jax.ShapeDtypeStruct((1, rows - 2, cells, channels), BF16)
    edge = jax.ShapeDtypeStruct((2, cells, channels), BF16)
    return acc, frame, inner, edge


def own(last, first, up, down, gain, k, token):
    acc = shapes()[0]
    args = [last, first, w(up), w(down), gain, k[1], k[2], (token, pl.BlockSpec(memory_space=pl.ANY))]
    return call(own_kernel, "own", 3, [whole(acc.shape)] * 2, [acc, acc], args)


def own_last(last, gain, k):
    acc = shapes()[0]
    return call(own_last_kernel, "last", 1, [whole(acc.shape)], [acc], [last, gain, k[2]])[0]


def own_first(first, up, down, gain, k, bias, latents, acc_last, token):
    acc = shapes()[0]
    up, down = pairs(up, 1), pairs(down, 1)
    args = [first, up[0], down[0], up[1], down[1], gain, k[1], k[2], bias]
    args += [(latents, part(latents.shape, 0)), w(acc_last), rest(token)]
    return call(own_first_kernel, "first", 2, [whole(acc.shape)] * 2, [acc, acc], args)


def inner_rows(latents, token):
    rows = latents.shape[1]
    inner = shapes()[2]

    def copy(last, first, _, last_out, first_out):
        last_out[...] = last[:, 1 : rows - 1]
        first_out[...] = first[:, 1 : rows - 1]

    return pl.pallas_call(
        copy,
        grid=(1,),
        in_specs=[part(latents.shape, 1), part(latents.shape, 0), pl.BlockSpec(memory_space=pl.ANY)],
        out_specs=[whole(inner.shape)] * 2,
        out_shape=[inner] * 2,
        compiler_params=pltpu.CompilerParams(vmem_limit_bytes=6 * 2**20),
        name="inner",
    )(latents, latents, token)


def rows_after(token, *sources, plain=False):
    count = len(sources)

    def copy(*refs):
        inward, outward, *rows = refs[2 * count + (token is not None) :]
        lower = lax.axis_index("height") % 2 == 0
        for n in range(count):
            top, bottom = (ref.reshape(inward.shape[1:])[...] for ref in refs[2 * n : 2 * n + 2])
            inward[n] = jnp.where(lower, bottom, top)
            outward[n] = jnp.where(lower, top, bottom)
            if plain:
                rows[0][2 * n] = top
                rows[0][2 * n + 1] = bottom

    args = []
    for array, *places in sources:
        for place in places:
            block = (1,) * len(place) + array.shape[len(place) :]
            tail = (0,) * (array.ndim - len(place))
            args.append((array, pl.BlockSpec(block, lambda i, p=place, t=tail: (*p, *t))))
    if token is not None:
        args.append((token, pl.BlockSpec(memory_space=pl.ANY)))
    row = sources[0][0].shape[-2:]
    outs = [jax.ShapeDtypeStruct((n, *row), BF16) for n in [count] * 2 + [2 * count] * plain]
    return pl.pallas_call(
        copy,
        grid=(1,),
        in_specs=[spec for _, spec in args],
        out_specs=[whole(o.shape) for o in outs],
        out_shape=outs,
        compiler_params=pltpu.CompilerParams(vmem_limit_bytes=4 * 2**20),
        name="edges",
    )(*[array for array, _ in args])


def pairs(array, size):
    block = (size, *array.shape[1:])
    return [
        (array, pl.BlockSpec(block, lambda i, n=n: (n,) + (0,) * (len(block) - 1)))
        for n in range(array.shape[0] // size)
    ]


def first_section(latents, gain, kernel, bias, ahead):
    bottom = latents.shape[1] - 1
    acc, frame, inner, edge = shapes()
    k = [(kernel, part(kernel.shape, i)) for i in range(3)]
    first, last = ((latents, part(latents.shape, i)) for i in range(2))
    sources = [(latents, (i, 0), (i, bottom)) for i in range(2)]
    edges = latents[:, ::bottom].reshape(4, *latents.shape[2:])
    sides = rows_after(None, *sources)
    edges = shift(edges)
    up, down = exchange_rows(*sides)
    inner_last, inner_first = inner_rows(latents, sides[0])
    before, earliest = shift(inner_last), shift(inner_first, False)

    sides = rows_after(up, (edges, (2,), (3,)), (edges, (0,), (1,)))
    acc_first, acc_last = own(last, first, up, down, gain, k, sides[0])
    up, down = (pairs(a, 1) for a in exchange_rows(*sides))
    edges = pairs(edges, 2)
    outs = [frame, acc]
    y_last, acc_first = call(
        functools.partial(before_kernel, False),
        "before",
        2,
        [whole(o.shape) for o in outs],
        outs,
        [w(before), edges[1], up[0], down[0], gain, k[0], k[1], bias, w(acc_first), w(acc_last)],
    )
    second_last = ahead(y_last)
    outs = [frame]
    (y_first,) = call(
        earliest_kernel,
        "earliest",
        1,
        [whole(o.shape) for o in outs],
        outs,
        [w(earliest), edges[0], up[1], down[1], gain, k[0], bias, w(acc_first), rest(second_last)],
    )
    return y_last, y_first, second_last


def second_section(results, latents, gain, kernel, bias):
    y_last, y_first, acc_last = results
    rows, cells, channels = latents.shape[1:]
    bottom = rows - 1
    acc, _, inner, edge = shapes()
    k = [(kernel, part(kernel.shape, i)) for i in range(3)]
    before = shift(y_last)
    frames = [(y, (0, 0), (0, bottom)) for y in (y_first, y_last)]
    up, down = exchange_rows(*rows_after(None, *frames))
    outs = [inner, jax.ShapeDtypeStruct(edge.shape, F32)]
    inner_ahead, edge_acc = call(
        ahead_kernel, "ahead", 1, [whole(o.shape) for o in outs], outs, [w(y_first), gain, k[0]]
    )
    inner_ahead = shift(inner_ahead)
    args = [pairs(up, 1)[0], pairs(down, 1)[0], gain, k[0], w(edge_acc), rest(acc_last)]
    columns = [pltpu.VMEM((cells, 3 * channels), BF16)]
    (edges_ahead,) = call(edges_kernel, "ends", 0, [whole(edge.shape)], [edge], args, scratch=columns)
    edges_ahead = shift(edges_ahead, False)
    sides = rows_after(up, (before, (0, 0), (0, bottom)))
    acc_first, acc_last = own_first(w(y_first), up, down, gain, k, bias, latents, acc_last, sides[0])

    out = jax.ShapeDtypeStruct(latents.shape, BF16)
    anywhere = pl.BlockSpec(memory_space=pl.ANY)
    extra = [pltpu.VMEM(latents.shape[1:], BF16), pltpu.SemaphoreType.DMA((2,))]
    flat = (rows + 2) * cells
    scratch = [
        pltpu.VMEM((3, flat, channels), F32),
        pltpu.VMEM((flat, 3 * channels), BF16),
        pltpu.VMEM((flat - 2 * cells, 3 * channels), BF16),
    ]
    args = [w(before), *map(w, exchange_rows(*sides)), gain, k[0], k[1], bias, w(acc_first), w(acc_last)]
    args.append((latents, part(latents.shape, 1)))
    half, acc_first = call(
        functools.partial(before_kernel, True),
        "before",
        2,
        [anywhere, whole(acc.shape)],
        [out, acc],
        args,
        scratch=scratch + extra,
    )
    args = [w(inner_ahead), w(edges_ahead), w(acc_first), rest(half)]
    return call(sum_kernel, "sum", 0, anywhere, out, args, {len(args) - 1: 0}, extra, 12 * 2**20)


def per_device(
    latents, first_gain, first_kernel, first_bias, second_gain, second_kernel, second_bias
):
    frames, rows, cells, channels = latents.shape
    call.block = (rows, cells, channels)

    def columns(kernel):
        return kernel.reshape(3, 3, 3 * channels, channels)

    first_gain, first_bias, second_gain, second_bias = map(w, (first_gain, first_bias, second_gain, second_bias))
    second_kernel = columns(second_kernel)
    k = [(second_kernel, part(second_kernel.shape, i)) for i in range(3)]

    def ahead(y_last):
        return own_last(w(y_last), second_gain, k)

    results = first_section(latents, first_gain, columns(first_kernel), first_bias, ahead)
    return second_section(results, latents, second_gain, second_kernel, second_bias)


def solution(mesh):
    return jax.shard_map(
        per_device,
        mesh=mesh,
        in_specs=(P("tm", "height", None, None), P(), P(), P(), P(), P(), P()),
        out_specs=P("tm", "height", None, None),
        check_vma=False,
    )
```
